512 devices in a mesh: grp: 16 (over z_lo, x), layer: 32 (over y, z_hi, core).
Axes of the slice: x: 4, y: 8, z: 8 (z_hi: 2, z_lo: 4; z = z_hi * 4 + z_lo), core: 2. Of those that a mesh axis runs over, the one named last changes fastest.
Arguments:
- grads: bfloat16 [32, 3072, 4096], P('layer', 'grp'), may hold values from -6 to 6
- in_factor: float32 [32, 64, 64], P('layer'), may hold values from -0.02 to 3, as said below
- out_factor: float32 [32, 64, 64], P('layer'), may hold values from -0.02 to 3, as said below
Outputs:
- scores: float32 [3072, 9, 192], P('grp', None, 'layer')
The draws below stay inside these ranges and needn't reach their ends.
Inputs may be any that keep to these rules, and one draw needn't show every extreme that they name: `in_factor`: each layer's matrix is symmetric, and every diagonal entry exceeds the sum of magnitudes of the other entries of its row. `out_factor`: each layer's matrix is symmetric, and every diagonal entry exceeds the sum of magnitudes of the other entries of its row.
All inputs are finite; a program needn't handle non-finite values.
Results may differ from the reference program's by a relative error of at most 0.00034.
Values may be sent and summed in bfloat16 or wider, within the bound.
No kernel may reach another device: no remote copies, remote signals or barrier semaphores. Data moves between devices by JAX's collectives and lax.ppermute only.
A program may use at most 64 MiB of HBM per device.

```python
import math
import jax
import jax.numpy as jnp
from jax import lax

K_IN = 64
K_OUT = 64
BLOCK = 192
LAYERS = 32
EXAMPLES = 3072
N_GRP = 16


def symmetric_matrix(key, diag_values, off_scale):
    order = diag_values.shape[-1]
    raw = jax.random.uniform(key, diag_values.shape + (order,), jnp.float32, -1.0, 1.0)
    off = off_scale * (raw + jnp.swapaxes(raw, -1, -2)) * 0.5
    eye = jnp.eye(order, dtype=jnp.float32)
    return off * (1.0 - eye) + eye * diag_values[..., None]


def draw_in_factor(key, part):
    key = jax.random.fold_in(key, 11)
    key_diag, key_off = jax.random.split(key)
    diag_values = jax.random.uniform(key_diag, (LAYERS, K_IN), jnp.float32, 1.5, 3.0)
    return symmetric_matrix(key_off, diag_values, 0.02)


def draw_out_factor(key, part):
    key = jax.random.fold_in(key, 23)
    key_diag, key_off = jax.random.split(key)
    diag_values = jax.random.uniform(key_diag, (LAYERS, K_OUT), jnp.float32, 1.5, 3.0)
    return symmetric_matrix(key_off, diag_values, 0.02)


def level_of(own_key, shape, shards, low, high):
    factor_of = 1.0
    for dim, shards_of in shards:
        heights = jax.random.uniform(jax.random.fold_in(jax.random.fold_in(own_key, 6), dim), (shards_of,), jnp.float32, low / len(shards), high / len(shards))
        factor_of = factor_of * jnp.repeat(jnp.exp(heights), shape[dim] // shards_of).reshape((-1,) + (1,) * (len(shape) - 1 - dim))
    return factor_of


def noise(own_key, shape, deviation, reach, cuts=(), kind=jnp.bfloat16):
    values = deviation * jax.random.normal(own_key, shape, jnp.float32)
    if cuts:
        values = values * level_of(own_key, shape, cuts, -0.22, 0.18)
    return jnp.clip(values, -reach, reach).astype(kind)


def setup_inputs(seed: int = 0) -> dict:
    key_list = jax.random.split(jax.random.key(seed), 4)
    grads = noise(key_list[0], (LAYERS, EXAMPLES, K_OUT * K_IN), 1.0, 6.0, ((0, 32), (1, 16)))
    in_factor = draw_in_factor(jax.random.fold_in(key_list[3], 71), 0)
    out_factor = draw_out_factor(jax.random.fold_in(key_list[3], 71), 0)
    return {"grads": grads, "in_factor": in_factor, "out_factor": out_factor}


def precondition(rows, in_mat, out_mat):
    matrix = rows.astype(jnp.float32).reshape(-1, K_OUT, K_IN)
    left = jnp.einsum('po,boi->bpi', out_mat, matrix, precision=lax.Precision.HIGHEST)
    right = jnp.einsum('bpi,iq->bpq', left, in_mat, precision=lax.Precision.HIGHEST)
    return right.reshape(-1, K_OUT * K_IN).astype(jnp.bfloat16)

def reference(grads, in_factor, out_factor):
    offsets = N_GRP // 2 + 1

    def layer_step(total, items):
        rows, in_mat, out_mat = items
        weighted = precondition(rows, in_mat, out_mat).astype(jnp.float32).reshape(N_GRP, BLOCK, -1)
        plain = rows.astype(jnp.float32).reshape(N_GRP, BLOCK, -1)
        blocks = []
        for offset in range(offsets):
            moved = jnp.roll(plain, -offset, axis=0)
            blocks.append(jnp.einsum('gik,gjk->gij', weighted, moved))
        return (total + jnp.stack(blocks, axis=2), None)
    start = jnp.zeros((N_GRP, BLOCK, offsets, BLOCK), jnp.float32)
    total, unused = lax.scan(layer_step, start, (grads, in_factor, out_factor))
    factor = 1.0 / math.sqrt(LAYERS * K_OUT * K_IN)
    return (total.reshape(EXAMPLES, offsets, BLOCK) * factor).astype(jnp.float32)
```

```python
import math

import jax
import jax.numpy as jnp
from jax import lax
from jax.sharding import Mesh, PartitionSpec as P

NZ, NX, NY, NH, NC = 4, 4, 8, 2, 2


def moved(value, axis, steps):
    count = lax.axis_size(axis)
    return lax.ppermute(value, axis, [(s, (s + steps) % count) for s in range(count)])


def precondition(rows, in_mat, out_mat):
    matrix = rows.astype(jnp.float32).reshape(-1, out_mat.shape[0], in_mat.shape[0])
    left = jnp.einsum("po,boi->bpi", out_mat, matrix, precision=lax.Precision.HIGHEST)
    right = jnp.einsum("bpi,iq->bpq", left, in_mat, precision=lax.Precision.HIGHEST)
    return right.astype(jnp.bfloat16).reshape(rows.shape)


def product(plain, weighted):
    return lax.dot_general(
        plain, weighted, (((1,), (1,)), ((), ())), preferred_element_type=jnp.float32
    )


def per_device(grads, in_factor, out_factor):
    _, rows, width = grads.shape
    factor = 1.0 / math.sqrt(32 * width)
    x = lax.axis_index("x")
    plain0 = grads[0]
    plain1 = moved(plain0, "zl", -1)
    plain2 = moved(plain0, "zl", -2)
    own = precondition(plain0, in_factor[0], out_factor[0])
    weighted = [own, moved(own, "x", 1), moved(own, "x", 2), moved(own, "x", 3)]
    next_row = [product(plain1, w) for w in weighted]
    chosen = [
        jnp.where(x >= r, product(plain0, weighted[r]), product(plain2, weighted[r]))
        for r in range(1, NX)
    ]
    ends = [product(plain0, own), product(plain2, own)]
    slots = jnp.concatenate(next_row + chosen + ends, axis=1)
    lanes = 1792
    slots = jnp.pad(slots, ((0, 0), (0, lanes - slots.shape[1])))
    half = lanes // 2
    pair = jnp.stack([slots[:, :half], slots[:, half:]])
    pair = lax.all_to_all(pair, "c", 0, 0, tiled=False)
    part = (pair[0] + pair[1]).reshape(NY, rows // NY, half)
    part = lax.all_to_all(part, "y", 0, 0, tiled=False).sum(0)
    part = part.reshape(NH * NC, rows // 32, half)
    part = lax.all_to_all(part, ("zh", "c"), 0, 0, tiled=False)
    part = part.reshape(NH, NC, rows // 32, half).sum(0)
    full = part.transpose(1, 0, 2).reshape(rows // 32, lanes)[:, : 9 * rows]
    full = full.reshape(rows // 32, 9, rows) * factor
    out = [None] * 9
    out[4], out[0], out[8] = full[:, 0], full[:, 7], full[:, 8]
    for r in range(1, NX):
        both = moved(jnp.stack([full[:, r], full[:, 3 + r]]), "x", -r)
        inside = x + r < NX
        out[r] = jnp.where(inside, both[1], both[0])
        out[r + 4] = jnp.where(inside, both[0], both[1])
    return jnp.stack(out).transpose(2, 0, 1)


def solution(mesh):
    fine = Mesh(mesh.devices.reshape(NZ, NX, NY, NH, NC), ("zl", "x", "y", "zh", "c"))
    layer, group = ("y", "zh", "c"), ("zl", "x")
    in_specs = (P(layer, group, None), P(layer, None, None), P(layer, None, None))
    return jax.shard_map(
        per_device, mesh=fine, in_specs=in_specs, out_specs=P(group, None, layer), check_vma=False
    )
```

```python
import functools
import math

import jax
import jax.numpy as jnp
import numpy as np
from jax import lax
from jax.experimental import pallas as pl
from jax.experimental.pallas import tpu as pltpu
from jax.sharding import Mesh, PartitionSpec as P

NZ, NX, NY, NH, NC = 4, 4, 8, 2, 2
NL = NY * NH
ROWS = 192
OWN = ROWS // (NL * NC)
LANES = 128
PIECE = OWN * ROWS // LANES
TILE = 256
NN, NT = ((1,), (0,)), ((1,), (1,))
COST = pl.CostEstimate(flops=10**10, bytes_accessed=10**6, transcendentals=0)


def moved(value, axis, steps):
    count = lax.axis_size(axis)
    return lax.ppermute(value, axis, [(s, (s + steps) % count) for s in range(count)])


def held_kernel(value_ref, *refs):
    pass


def held(value, *others):
    anywhere = pl.BlockSpec(memory_space=pl.ANY)
    return pl.pallas_call(
        held_kernel,
        out_shape=jax.ShapeDtypeStruct(value.shape, value.dtype),
        in_specs=[anywhere] * (1 + len(others)),
        out_specs=anywhere,
        input_output_aliases={0: 0},
        cost_estimate=COST,
    )(value, *others)


def spread():
    at = np.arange(TILE)
    six = np.arange(64)
    by_four = (at[:, None] // 4 == six).astype(np.float32)
    by_last = (at[:, None] % 64 == six).astype(np.float32)
    mixed = (at[:, None] // 16 * 4 + at[:, None] % 4 == six).astype(np.float32)
    inner = (at[:, None] % 4 == at // 64).astype(np.float32)
    outer = (at[:, None] // 4 % 4 == at // 4 % 4).astype(np.float32)
    order = np.zeros((TILE, TILE), np.float32)
    order[at, at % 64 * 4 + at // 64] = 1
    return [jnp.asarray(m) for m in (by_four, by_last, mixed, inner, outer)], jnp.asarray(
        order, jnp.bfloat16
    )


def tiles_kernel(in_ref, out_ref, four_ref, last_ref, mixed_ref, im_ref, om_ref, a_ref, b_ref):
    def exact(a, b, dims):
        return lax.dot_general(
            a,
            b,
            (dims, ((), ())),
            precision=lax.Precision.HIGHEST,
            preferred_element_type=jnp.float32,
        )

    def parts(ref, matrix):
        for part in range(3):
            rounded = matrix.astype(jnp.bfloat16)
            ref[:, part * TILE : (part + 1) * TILE] = rounded
            matrix = matrix - rounded.astype(jnp.float32)

    inner = exact(exact(four_ref[...], in_ref[...], NT), last_ref[...], NT)
    parts(a_ref, inner * im_ref[...])
    outer = exact(exact(mixed_ref[...], out_ref[...], NN), mixed_ref[...], NT)
    parts(b_ref, outer * om_ref[...])


def factor_tiles(in_mat, out_mat):
    matrices, order = spread()
    shape = jax.ShapeDtypeStruct((TILE, 3 * TILE), jnp.bfloat16)
    inner, outer = pl.pallas_call(
        tiles_kernel, out_shape=(shape, shape), cost_estimate=COST
    )(in_mat, out_mat, *matrices)
    return inner, outer, order


def dot(a, b, dims):
    return lax.dot_general(a, b, (dims, ((), ())), preferred_element_type=jnp.float32)


def weigh_kernel(p_ref, inner_ref, outer_ref, order_ref, w_ref, t_ref):
    tiles = p_ref.shape[1] // TILE

    @pl.loop(0, tiles, unroll=tiles)
    def _(b):
        x = p_ref[:, pl.ds(pl.multiple_of(b * TILE, TILE), TILE)]
        t_ref[b] = dot(inner_ref[...], jnp.concatenate([x] * 3, axis=1), NT)

    @pl.loop(0, tiles, unroll=tiles)
    def _(g):
        at = pl.ds(pl.multiple_of(g * 16, 16), 16)
        x = t_ref[:, at, :].reshape(TILE, ROWS)
        high = x.astype(jnp.bfloat16)
        low = (x - high.astype(jnp.float32)).astype(jnp.bfloat16)
        left = jnp.concatenate([outer_ref[:, : 2 * TILE], outer_ref[:, :TILE]], axis=1)
        y = dot(left, jnp.concatenate([high, high, low], axis=0), NN)
        t_ref[:, at, :] = y.reshape(16, 16, ROWS)

    @pl.loop(0, tiles, unroll=tiles)
    def _(b):
        y = dot(order_ref[...], t_ref[b].astype(jnp.bfloat16), NN)
        w_ref[pl.ds(pl.multiple_of(b * TILE, TILE), TILE), :] = y.astype(jnp.bfloat16)


def weigh(rows, tiles):
    width = rows.shape[1]
    return pl.pallas_call(
        weigh_kernel,
        out_shape=jax.ShapeDtypeStruct((width, ROWS), jnp.bfloat16),
        scratch_shapes=[pltpu.VMEM((width // TILE, TILE, ROWS), jnp.float32)],
        compiler_params=pltpu.CompilerParams(vmem_limit_bytes=24 * 2**20),
        cost_estimate=COST,
    )(rows, *tiles)


def products_kernel(picks, n_p, n_w, first, place_ref, *refs):
    p_refs, w_refs = refs[:n_p], refs[n_p : n_p + n_w]
    given, (out_ref, total) = refs[n_p + n_w : -2], refs[-2:]

    def score(slot, p, w):
        total[slot] = dot(p_refs[p][...], w_refs[w][...], NN)

    for slot, (axis, least, below, reached) in enumerate(picks):
        if axis is None:
            score(slot, *reached)
        else:
            here = place_ref[axis]
            pl.when(here < least)(functools.partial(score, slot, *below))
            pl.when(here >= least)(functools.partial(score, slot, *reached))
    if given:
        out_ref[:, :, : first * PIECE] = given[0][:, :, : first * PIECE]
    for pair in range(len(picks) // 2):
        a, b = total[2 * pair], total[2 * pair + 1]
        rest = jnp.concatenate([a[:, LANES:], b[:, LANES:]], axis=1)
        for n, piece in enumerate((a[:, :LANES], b[:, :LANES], rest)):
            to = first * PIECE + (3 * pair + n) * OWN
            for chip in range(NL):
                for core in range(NC):
                    at = (chip * NC + core) * OWN
                    out_ref[core, chip, to : to + OWN] = piece[at : at + OWN]


def products(plains, weights, picks, slots, first=0, sums=None):
    place = jnp.stack([lax.axis_index("zl"), lax.axis_index("x")]).astype(jnp.int32)
    given = () if sums is None else (sums,)
    vmem = pl.BlockSpec(memory_space=pltpu.VMEM)
    height = -(-slots * PIECE // 8) * 8
    return pl.pallas_call(
        functools.partial(products_kernel, picks, len(plains), len(weights), first),
        out_shape=jax.ShapeDtypeStruct((NC, NL, height, LANES), jnp.float32),
        in_specs=[pl.BlockSpec(memory_space=pltpu.SMEM)]
        + [vmem] * (len(plains) + len(weights) + len(given)),
        out_specs=vmem,
        scratch_shapes=[pltpu.VMEM((len(picks), ROWS, ROWS), jnp.float32)],
        compiler_params=pltpu.CompilerParams(vmem_limit_bytes=24 * 2**20),
        cost_estimate=COST,
    )(place, *plains, *weights, *given)


def unpacked(part, slots):
    part = part[: slots * PIECE].reshape(slots // 2, 3, OWN, LANES)
    rest = part[:, 2].reshape(slots // 2, OWN, 2, ROWS - LANES).transpose(0, 2, 1, 3)
    return jnp.concatenate([part[:, :2], rest], axis=-1).reshape(slots, OWN, ROWS)


def per_device(grads, in_factor, out_factor):
    factor = 1.0 / math.sqrt(NL * NC * grads.shape[-1])
    z, x = lax.axis_index("zl"), lax.axis_index("x")
    tiles = factor_tiles(in_factor[0], out_factor[0])
    half = ROWS // 2
    p0 = grads[0]
    p1, p3 = moved(p0, "x", 1), moved(p0, "x", -1)
    p4 = lax.ppermute(p0, "zl", [(0, 2), (3, 1), (1, 0)])
    own = held(p0, p4)
    p5 = lax.ppermute(own, "zl", [(0, 3), (2, 1), (3, 2)])
    p2 = jnp.concatenate([moved(p1[:half], "x", 1), moved(p3[half:], "x", -1)])
    w0, w1, w2, w3, w4 = (weigh(p, tiles) for p in (p0, p1, p2, p3, p4))
    early = products(
        [own, p1, p2, p3, p4],
        [w0, w1, w2, w3, w4],
        [
            (None, 0, None, (0, 0)),
            (1, 1, (1, 0), (0, 1)),
            (None, 0, None, (0, 2)),
            (None, 0, None, (4, 0)),
            (1, 1, (4, 1), (1, 4)),
            (1, 2, (4, 2), (2, 4)),
            (1, 3, (4, 3), (3, 4)),
            (None, 0, None, (0, 4)),
        ],
        12,
    )
    sums = products(
        [p4, p5], [w0, w1, w2, w3], [(0, 1, (0, r), (1, r)) for r in range(NX)], 12, 8, early
    )
    pair = lax.all_to_all(sums, "c", 0, 0, tiled=False)
    part = pair[0] + pair[1]
    part = lax.all_to_all(part, ("y", "zh"), 0, 0, tiled=False).sum(0)
    slots = unpacked(part, 12)
    row, two, again, following = slots[:3], slots[3:7], slots[7], slots[8:]
    out = [None] * 9
    out[0], out[4] = row[0], following[0]
    across = lax.ppermute(
        jnp.concatenate([again[None], two[1:]]), "zl", [(1, 3), (2, 0)]
    )
    middle = (z == 1) | (z == 2)
    out[8] = jnp.where(middle, two[0], across[0])
    for r in range(1, NX):
        same = row[r] if r < 3 else row[1]
        back = moved(jnp.stack([following[r], jnp.where(x >= r, same, two[r])]), "x", -r)
        inside = x + r < NX
        near = row[1] if r == 3 else back[1]
        far = jnp.where(middle, back[1], across[NX - r])
        out[r] = jnp.where(inside, near, back[0])
        out[r + 4] = jnp.where(inside, back[0], far)
    return (jnp.stack(out) * factor).transpose(2, 0, 1)


def solution(mesh):
    fine = Mesh(mesh.devices.reshape(NZ, NX, NY, NH, NC), ("zl", "x", "y", "zh", "c"))
    layer, group = ("y", "zh", "c"), ("zl", "x")
    in_specs = (P(layer, group, None), P(layer, None, None), P(layer, None, None))
    return jax.shard_map(
        per_device, mesh=fine, in_specs=in_specs, out_specs=P(group, None, layer), check_vma=False
    )
```

```python
import functools
import math

import jax
import jax.numpy as jnp
import numpy as np
from jax import lax
from jax.experimental import pallas as pl
from jax.experimental.pallas import tpu as pltpu
from jax.sharding import Mesh, PartitionSpec as P

NZ, NX, NY, NH, NC = 4, 4, 8, 2, 2
NL = NY * NH
ROWS = 192
OWN = ROWS // (NL * NC)
LANES = 128
PIECE = OWN * ROWS // LANES
TILE = 256
NN, NT = ((1,), (0,)), ((1,), (1,))
COST = pl.CostEstimate(flops=10**10, bytes_accessed=10**6, transcendentals=0)


def moved(value, axis, steps):
    count = lax.axis_size(axis)
    return lax.ppermute(value, axis, [(s, (s + steps) % count) for s in range(count)])


def spread():
    at = np.arange(TILE)
    six = np.arange(64)
    by_four = (at[:, None] // 4 == six).astype(np.float32)
    by_last = (at[:, None] % 64 == six).astype(np.float32)
    mixed = (at[:, None] // 16 * 4 + at[:, None] % 4 == six).astype(np.float32)
    inner = (at[:, None] % 4 == at // 64).astype(np.float32)
    outer = (at[:, None] // 4 % 4 == at // 4 % 4).astype(np.float32)
    order = np.zeros((TILE, TILE), np.float32)
    order[at, at % 64 * 4 + at // 64] = 1
    return [jnp.asarray(m) for m in (by_four, by_last, mixed, inner, outer)], jnp.asarray(
        order, jnp.bfloat16
    )


def tiles_kernel(in_ref, out_ref, four_ref, last_ref, mixed_ref, im_ref, om_ref, a_ref, b_ref):
    def exact(a, b, dims):
        return lax.dot_general(
            a,
            b,
            (dims, ((), ())),
            precision=lax.Precision.HIGHEST,
            preferred_element_type=jnp.float32,
        )

    def parts(ref, matrix):
        for part in range(3):
            rounded = matrix.astype(jnp.bfloat16)
            ref[:, part * TILE : (part + 1) * TILE] = rounded
            matrix = matrix - rounded.astype(jnp.float32)

    inner = exact(exact(four_ref[...], in_ref[...], NT), last_ref[...], NT)
    parts(a_ref, inner * im_ref[...])
    outer = exact(exact(mixed_ref[...], out_ref[...], NN), mixed_ref[...], NT)
    parts(b_ref, outer * om_ref[...])


def factor_tiles(in_mat, out_mat):
    matrices, order = spread()
    shape = jax.ShapeDtypeStruct((TILE, 3 * TILE), jnp.bfloat16)
    inner, outer = pl.pallas_call(
        tiles_kernel, out_shape=(shape, shape), cost_estimate=COST
    )(in_mat, out_mat, *matrices)
    return inner, outer, order


def dot(a, b, dims):
    return lax.dot_general(a, b, (dims, ((), ())), preferred_element_type=jnp.float32)


def weigh_kernel(p_ref, inner_ref, outer_ref, order_ref, w_ref, *rest):
    *copies, t_ref = rest
    tiles = p_ref.shape[1] // TILE
    for copy in copies:
        copy[...] = p_ref[...]

    @pl.loop(0, tiles, unroll=tiles)
    def _(b):
        x = p_ref[:, pl.ds(pl.multiple_of(b * TILE, TILE), TILE)]
        t_ref[b] = dot(inner_ref[...], jnp.concatenate([x] * 3, axis=1), NT)

    @pl.loop(0, tiles, unroll=tiles)
    def _(g):
        at = pl.ds(pl.multiple_of(g * 16, 16), 16)
        x = t_ref[:, at, :].reshape(TILE, ROWS)
        high = x.astype(jnp.bfloat16)
        low = (x - high.astype(jnp.float32)).astype(jnp.bfloat16)
        left = jnp.concatenate([outer_ref[:, : 2 * TILE], outer_ref[:, :TILE]], axis=1)
        y = dot(left, jnp.concatenate([high, high, low], axis=0), NN)
        t_ref[:, at, :] = y.reshape(16, 16, ROWS)

    @pl.loop(0, tiles, unroll=tiles)
    def _(b):
        y = dot(order_ref[...], t_ref[b].astype(jnp.bfloat16), NN)
        w_ref[pl.ds(pl.multiple_of(b * TILE, TILE), TILE), :] = y.astype(jnp.bfloat16)


def weigh(rows, tiles, copied=False):
    width = rows.shape[1]
    out = jax.ShapeDtypeStruct((width, ROWS), jnp.bfloat16)
    return pl.pallas_call(
        weigh_kernel,
        out_shape=(out, jax.ShapeDtypeStruct(rows.shape, rows.dtype)) if copied else out,
        scratch_shapes=[pltpu.VMEM((width // TILE, TILE, ROWS), jnp.float32)],
        compiler_params=pltpu.CompilerParams(vmem_limit_bytes=24 * 2**20),
        cost_estimate=COST,
    )(rows, *tiles)


def products_kernel(picks, n_p, n_w, first, place_ref, *refs):
    p_refs, w_refs = refs[:n_p], refs[n_p : n_p + n_w]
    given, (out_ref, total) = refs[n_p + n_w : -2], refs[-2:]

    def score(slot, p, w):
        total[slot] = dot(p_refs[p][...], w_refs[w][...], NN)

    for slot, (axis, least, below, reached) in enumerate(picks):
        if axis is None:
            score(slot, *reached)
        else:
            here = place_ref[axis]
            pl.when(here < least)(functools.partial(score, slot, *below))
            pl.when(here >= least)(functools.partial(score, slot, *reached))
    if given:
        out_ref[:, :, : first * PIECE] = given[0][:, :, : first * PIECE]
    for pair in range(len(picks) // 2):
        a, b = total[2 * pair], total[2 * pair + 1]
        rest = jnp.concatenate([a[:, LANES:], b[:, LANES:]], axis=1)
        for n, piece in enumerate((a[:, :LANES], b[:, :LANES], rest)):
            to = first * PIECE + (3 * pair + n) * OWN
            for chip in range(NL):
                for core in range(NC):
                    at = (chip * NC + core) * OWN
                    out_ref[core, chip, to : to + OWN] = piece[at : at + OWN]


def products(plains, weights, picks, slots, first=0, sums=None):
    place = jnp.stack([lax.axis_index("zl"), lax.axis_index("x")]).astype(jnp.int32)
    given = () if sums is None else (sums,)
    vmem = pl.BlockSpec(memory_space=pltpu.VMEM)
    height = -(-slots * PIECE // 8) * 8
    return pl.pallas_call(
        functools.partial(products_kernel, picks, len(plains), len(weights), first),
        out_shape=jax.ShapeDtypeStruct((NC, NL, height, LANES), jnp.float32),
        in_specs=[pl.BlockSpec(memory_space=pltpu.SMEM)]
        + [vmem] * (len(plains) + len(weights) + len(given)),
        out_specs=vmem,
        scratch_shapes=[pltpu.VMEM((len(picks), ROWS, ROWS), jnp.float32)],
        compiler_params=pltpu.CompilerParams(vmem_limit_bytes=24 * 2**20),
        cost_estimate=COST,
    )(place, *plains, *weights, *given)


def unpacked(part, slots):
    part = part[: slots * PIECE].reshape(slots // 2, 3, OWN, LANES)
    rest = part[:, 2].reshape(slots // 2, OWN, 2, ROWS - LANES).transpose(0, 2, 1, 3)
    return jnp.concatenate([part[:, :2], rest], axis=-1).reshape(slots, OWN, ROWS)


def per_device(grads, in_factor, out_factor):
    factor = 1.0 / math.sqrt(NL * NC * grads.shape[-1])
    z, x = lax.axis_index("zl"), lax.axis_index("x")
    tiles = factor_tiles(in_factor[0], out_factor[0])
    half = ROWS // 2
    p0 = grads[0]
    p1, p3 = moved(p0, "x", 1), moved(p0, "x", -1)
    p4 = lax.ppermute(p0, "zl", [(0, 2), (3, 1), (1, 0)])
    w0, own = weigh(p0, tiles, copied=True)
    p5 = lax.ppermute(own, "zl", [(0, 3), (2, 1), (3, 2)])
    p2 = jnp.concatenate([moved(p1[:half], "x", 1), moved(p3[half:], "x", -1)])
    w1, w2, w3, w4 = (weigh(p, tiles) for p in (p1, p2, p3, p4))
    early = products(
        [own, p1, p2, p3, p4],
        [w0, w1, w2, w3, w4],
        [
            (None, 0, None, (0, 0)),
            (1, 1, (1, 0), (0, 1)),
            (None, 0, None, (0, 2)),
            (None, 0, None, (4, 0)),
            (1, 1, (4, 1), (1, 4)),
            (1, 2, (4, 2), (2, 4)),
            (1, 3, (4, 3), (3, 4)),
            (None, 0, None, (0, 4)),
        ],
        12,
    )
    sums = products(
        [p4, p5], [w0, w1, w2, w3], [(0, 1, (0, r), (1, r)) for r in range(NX)], 12, 8, early
    )
    pair = lax.all_to_all(sums, "c", 0, 0, tiled=False)
    part = pair[0] + pair[1]
    part = lax.all_to_all(part, ("y", "zh"), 0, 0, tiled=False).sum(0)
    slots = unpacked(part, 12)
    row, two, again, following = slots[:3], slots[3:7], slots[7], slots[8:]
    out = [None] * 9
    out[0], out[4] = row[0], following[0]
    across = lax.ppermute(
        jnp.concatenate([again[None], two[1:]]), "zl", [(1, 3), (2, 0)]
    )
    middle = (z == 1) | (z == 2)
    out[8] = jnp.where(middle, two[0], across[0])
    for r in range(1, NX):
        same = row[r] if r < 3 else row[1]
        back = moved(jnp.stack([following[r], jnp.where(x >= r, same, two[r])]), "x", -r)
        inside = x + r < NX
        near = row[1] if r == 3 else back[1]
        far = jnp.where(middle, back[1], across[NX - r])
        out[r] = jnp.where(inside, near, back[0])
        out[r + 4] = jnp.where(inside, back[0], far)
    return (jnp.stack(out) * factor).transpose(2, 0, 1)


def solution(mesh):
    fine = Mesh(mesh.devices.reshape(NZ, NX, NY, NH, NC), ("zl", "x", "y", "zh", "c"))
    layer, group = ("y", "zh", "c"), ("zl", "x")
    in_specs = (P(layer, group, None), P(layer, None, None), P(layer, None, None))
    return jax.shard_map(
        per_device, mesh=fine, in_specs=in_specs, out_specs=P(group, None, layer), check_vma=False
    )
```

```python
import functools
import math

import jax
import jax.numpy as jnp
import numpy as np
from jax import lax
from jax.experimental import pallas as pl
from jax.experimental.pallas import tpu as pltpu
from jax.sharding import Mesh, PartitionSpec as P

NZ, NX, NY, NH, NC = 4, 4, 8, 2, 2
NL = NY * NH
ROWS = 192
OWN = ROWS // (NL * NC)
LANES = 128
PIECE = OWN * ROWS // LANES
TILE = 256
NN, NT = ((1,), (0,)), ((1,), (1,))
COST = pl.CostEstimate(flops=10**10, bytes_accessed=10**6, transcendentals=0)


def moved(value, axis, steps):
    count = lax.axis_size(axis)
    return lax.ppermute(value, axis, [(s, (s + steps) % count) for s in range(count)])


def spread():
    at = np.arange(TILE)
    six = np.arange(64)
    by_four = (at[:, None] // 4 == six).astype(np.float32)
    by_last = (at[:, None] % 64 == six).astype(np.float32)
    mixed = (at[:, None] // 16 * 4 + at[:, None] % 4 == six).astype(np.float32)
    inner = (at[:, None] % 4 == at // 64).astype(np.float32)
    outer = (at[:, None] // 4 % 4 == at // 4 % 4).astype(np.float32)
    order = np.zeros((TILE, TILE), np.float32)
    order[at, at % 64 * 4 + at // 64] = 1
    return [jnp.asarray(m) for m in (by_four, by_last, mixed, inner, outer)], jnp.asarray(
        order, jnp.bfloat16
    )


def tiles_kernel(in_ref, out_ref, four_ref, last_ref, mixed_ref, im_ref, om_ref, a_ref, b_ref):
    def exact(a, b, dims):
        return lax.dot_general(
            a,
            b,
            (dims, ((), ())),
            precision=lax.Precision.HIGHEST,
            preferred_element_type=jnp.float32,
        )

    def parts(ref, matrix):
        for part in range(3):
            rounded = matrix.astype(jnp.bfloat16)
            ref[:, part * TILE : (part + 1) * TILE] = rounded
            matrix = matrix - rounded.astype(jnp.float32)

    inner = exact(exact(four_ref[...], in_ref[...], NT), last_ref[...], NT)
    parts(a_ref, inner * im_ref[...])
    outer = exact(exact(mixed_ref[...], out_ref[...], NN), mixed_ref[...], NT)
    parts(b_ref, outer * om_ref[...])


def factor_tiles(in_mat, out_mat):
    matrices, order = spread()
    shape = jax.ShapeDtypeStruct((TILE, 3 * TILE), jnp.bfloat16)
    inner, outer = pl.pallas_call(
        tiles_kernel, out_shape=(shape, shape), cost_estimate=COST
    )(in_mat, out_mat, *matrices)
    return inner, outer, order


def dot(a, b, dims):
    return lax.dot_general(a, b, (dims, ((), ())), preferred_element_type=jnp.float32)


def weigh_kernel(p_ref, inner_ref, outer_ref, order_ref, w_ref, *rest):
    *copies, t_ref = rest
    tiles = p_ref.shape[1] // TILE
    for copy in copies:
        copy[...] = p_ref[...]

    @pl.loop(0, tiles, unroll=tiles)
    def _(b):
        x = p_ref[:, pl.ds(pl.multiple_of(b * TILE, TILE), TILE)]
        t_ref[b] = dot(inner_ref[...], jnp.concatenate([x] * 3, axis=1), NT)

    @pl.loop(0, tiles, unroll=tiles)
    def _(g):
        at = pl.ds(pl.multiple_of(g * 16, 16), 16)
        x = t_ref[:, at, :].reshape(TILE, ROWS)
        high = x.astype(jnp.bfloat16)
        low = (x - high.astype(jnp.float32)).astype(jnp.bfloat16)
        left = jnp.concatenate([outer_ref[:, : 2 * TILE], outer_ref[:, :TILE]], axis=1)
        y = dot(left, jnp.concatenate([high, high, low], axis=0), NN)
        t_ref[:, at, :] = y.reshape(16, 16, ROWS)

    @pl.loop(0, tiles, unroll=tiles)
    def _(b):
        y = dot(order_ref[...], t_ref[b].astype(jnp.bfloat16), NN)
        w_ref[pl.ds(pl.multiple_of(b * TILE, TILE), TILE), :] = y.astype(jnp.bfloat16)


def weigh(rows, tiles, copied=False):
    width = rows.shape[1]
    out = jax.ShapeDtypeStruct((width, ROWS), jnp.bfloat16)
    return pl.pallas_call(
        weigh_kernel,
        out_shape=(out, jax.ShapeDtypeStruct(rows.shape, rows.dtype)) if copied else out,
        scratch_shapes=[pltpu.VMEM((width // TILE, TILE, ROWS), jnp.float32)],
        compiler_params=pltpu.CompilerParams(vmem_limit_bytes=24 * 2**20),
        cost_estimate=COST,
    )(rows, *tiles)


def products_kernel(picks, n_p, n_w, first, place_ref, *refs):
    p_refs, w_refs = refs[:n_p], refs[n_p : n_p + n_w]
    given, (out_ref, total) = refs[n_p + n_w : -2], refs[-2:]

    def score(slot, p, w):
        total[slot] = dot(p_refs[p][...], w_refs[w][...], NN)

    for slot, (axis, least, below, reached) in enumerate(picks):
        if axis is None:
            score(slot, *reached)
        else:
            here = place_ref[axis]
            pl.when(here < least)(functools.partial(score, slot, *below))
            pl.when(here >= least)(functools.partial(score, slot, *reached))
    if given:
        before = given[0][:, :, : first * PIECE]
        out_ref[:, :, : first * PIECE] = before
        top = jnp.maximum(jnp.max(jnp.abs(before)), jnp.max(jnp.abs(total[...])))
        end = (first + len(picks)) * PIECE
        left = out_ref.shape[2] - end
        out_ref[:, :, end:] = jnp.full((NC, NL, left, LANES), top, jnp.float32)
    for pair in range(len(picks) // 2):
        a, b = total[2 * pair], total[2 * pair + 1]
        rest = jnp.concatenate([a[:, LANES:], b[:, LANES:]], axis=1)
        for n, piece in enumerate((a[:, :LANES], b[:, :LANES], rest)):
            to = first * PIECE + (3 * pair + n) * OWN
            for chip in range(NL):
                for core in range(NC):
                    at = (chip * NC + core) * OWN
                    out_ref[core, chip, to : to + OWN] = piece[at : at + OWN]


def products(plains, weights, picks, slots, first=0, sums=None):
    place = jnp.stack([lax.axis_index("zl"), lax.axis_index("x")]).astype(jnp.int32)
    given = () if sums is None else (sums,)
    vmem = pl.BlockSpec(memory_space=pltpu.VMEM)
    height = -(-slots * PIECE // 8) * 8
    return pl.pallas_call(
        functools.partial(products_kernel, picks, len(plains), len(weights), first),
        out_shape=jax.ShapeDtypeStruct((NC, NL, height, LANES), jnp.float32),
        in_specs=[pl.BlockSpec(memory_space=pltpu.SMEM)]
        + [vmem] * (len(plains) + len(weights) + len(given)),
        out_specs=vmem,
        scratch_shapes=[pltpu.VMEM((len(picks), ROWS, ROWS), jnp.float32)],
        compiler_params=pltpu.CompilerParams(vmem_limit_bytes=24 * 2**20),
        cost_estimate=COST,
    )(place, *plains, *weights, *given)


def unpacked(part, slots):
    part = part[: slots * PIECE].reshape(slots // 2, 3, OWN, LANES)
    rest = part[:, 2].reshape(slots // 2, OWN, 2, ROWS - LANES).transpose(0, 2, 1, 3)
    return jnp.concatenate([part[:, :2], rest], axis=-1).reshape(slots, OWN, ROWS)


def layer_sum(pair, end):
    bound = jnp.maximum(pair[0, 0, end, 0] + pair[1, 0, end, 0], 1e-30)
    power = jnp.floor(jnp.log2(bound)) - 14
    scaled = (pair[0, :, :end] + pair[1, :, :end]) * jnp.exp2(-power)
    powers = jnp.full((NL, pair.shape[2] - end, LANES), power, jnp.float32)
    sent = jnp.concatenate([scaled, powers], axis=1).astype(jnp.float16)
    got = lax.all_to_all(sent, ("y", "zh"), 0, 0, tiled=False).astype(jnp.float32)
    return (got[:, :end] * jnp.exp2(got[:, end : end + 1, :1])).sum(0)


def per_device(grads, in_factor, out_factor):
    factor = 1.0 / math.sqrt(NL * NC * grads.shape[-1])
    z, x = lax.axis_index("zl"), lax.axis_index("x")
    tiles = factor_tiles(in_factor[0], out_factor[0])
    half = ROWS // 2
    p0 = grads[0]
    p1, p3 = moved(p0, "x", 1), moved(p0, "x", -1)
    p4 = lax.ppermute(p0, "zl", [(0, 2), (3, 1), (1, 0)])
    w0, own = weigh(p0, tiles, copied=True)
    p5 = lax.ppermute(own, "zl", [(0, 3), (2, 1), (3, 2)])
    p2 = jnp.concatenate([moved(p1[:half], "x", 1), moved(p3[half:], "x", -1)])
    w1, w2, w3, w4 = (weigh(p, tiles) for p in (p1, p2, p3, p4))
    early = products(
        [own, p1, p2, p3, p4],
        [w0, w1, w2, w3, w4],
        [
            (None, 0, None, (0, 0)),
            (1, 1, (1, 0), (0, 1)),
            (None, 0, None, (0, 2)),
            (None, 0, None, (4, 0)),
            (1, 1, (4, 1), (1, 4)),
            (1, 2, (4, 2), (2, 4)),
            (1, 3, (4, 3), (3, 4)),
            (None, 0, None, (0, 4)),
        ],
        12,
    )
    sums = products(
        [p4, p5], [w0, w1, w2, w3], [(0, 1, (0, r), (1, r)) for r in range(NX)], 12, 8, early
    )
    pair = lax.all_to_all(sums, "c", 0, 0, tiled=False)
    slots = unpacked(layer_sum(pair, 12 * PIECE), 12)
    row, two, again, following = slots[:3], slots[3:7], slots[7], slots[8:]
    out = [None] * 9
    out[0], out[4] = row[0], following[0]
    across = lax.ppermute(
        jnp.concatenate([again[None], two[1:]]), "zl", [(1, 3), (2, 0)]
    )
    middle = (z == 1) | (z == 2)
    out[8] = jnp.where(middle, two[0], across[0])
    for r in range(1, NX):
        same = row[r] if r < 3 else row[1]
        back = moved(jnp.stack([following[r], jnp.where(x >= r, same, two[r])]), "x", -r)
        inside = x + r < NX
        near = row[1] if r == 3 else back[1]
        far = jnp.where(middle, back[1], across[NX - r])
        out[r] = jnp.where(inside, near, back[0])
        out[r + 4] = jnp.where(inside, back[0], far)
    return (jnp.stack(out) * factor).transpose(2, 0, 1)


def solution(mesh):
    fine = Mesh(mesh.devices.reshape(NZ, NX, NY, NH, NC), ("zl", "x", "y", "zh", "c"))
    layer, group = ("y", "zh", "c"), ("zl", "x")
    in_specs = (P(layer, group, None), P(layer, None, None), P(layer, None, None))
    return jax.shard_map(
        per_device, mesh=fine, in_specs=in_specs, out_specs=P(group, None, layer), check_vma=False
    )
```

```python
import functools
import math

import jax
import jax.numpy as jnp
import numpy as np
from jax import lax
from jax.experimental import pallas as pl
from jax.experimental.pallas import tpu as pltpu
from jax.sharding import Mesh, PartitionSpec as P

NZ, NX, NY, NH, NC = 4, 4, 8, 2, 2
NL = NY * NH
ROWS = 192
OWN = ROWS // (NL * NC)
LANES = 128
PIECE = OWN * ROWS // LANES
TILE = 256
NN, NT = ((1,), (0,)), ((1,), (1,))
COST = pl.CostEstimate(flops=10**10, bytes_accessed=10**6, transcendentals=0)


def moved(value, axis, steps):
    count = lax.axis_size(axis)
    return lax.ppermute(value, axis, [(s, (s + steps) % count) for s in range(count)])


def spread():
    at = np.arange(TILE)
    six = np.arange(64)
    by_four = (at[:, None] // 4 == six).astype(np.float32)
    by_last = (at[:, None] % 64 == six).astype(np.float32)
    mixed = (at[:, None] // 16 * 4 + at[:, None] % 4 == six).astype(np.float32)
    inner = (at[:, None] % 4 == at // 64).astype(np.float32)
    outer = (at[:, None] // 4 % 4 == at // 4 % 4).astype(np.float32)
    order = np.zeros((TILE, TILE), np.float32)
    order[at, at % 64 * 4 + at // 64] = 1
    return [jnp.asarray(m) for m in (by_four, by_last, mixed, inner, outer)], jnp.asarray(
        order, jnp.bfloat16
    )


def tiles_kernel(in_ref, out_ref, four_ref, last_ref, mixed_ref, im_ref, om_ref, a_ref, b_ref):
    def exact(a, b, dims):
        return lax.dot_general(
            a,
            b,
            (dims, ((), ())),
            precision=lax.Precision.HIGHEST,
            preferred_element_type=jnp.float32,
        )

    def parts(ref, matrix):
        for part in range(3):
            rounded = matrix.astype(jnp.bfloat16)
            ref[:, part * TILE : (part + 1) * TILE] = rounded
            matrix = matrix - rounded.astype(jnp.float32)

    inner = exact(exact(four_ref[...], in_ref[...], NT), last_ref[...], NT)
    parts(a_ref, inner * im_ref[...])
    outer = exact(exact(mixed_ref[...], out_ref[...], NN), mixed_ref[...], NT)
    parts(b_ref, outer * om_ref[...])


def factor_tiles(in_mat, out_mat):
    matrices, order = spread()
    shape = jax.ShapeDtypeStruct((TILE, 3 * TILE), jnp.bfloat16)
    inner, outer = pl.pallas_call(
        tiles_kernel, out_shape=(shape, shape), cost_estimate=COST
    )(in_mat, out_mat, *matrices)
    return inner, outer, order


def dot(a, b, dims):
    return lax.dot_general(a, b, (dims, ((), ())), preferred_element_type=jnp.float32)


def weigh_kernel(p_ref, inner_ref, outer_ref, order_ref, w_ref, *rest):
    *copies, t_ref = rest
    tiles = p_ref.shape[1] // TILE
    for copy in copies:
        copy[...] = p_ref[...]

    @pl.loop(0, tiles, unroll=tiles)
    def _(b):
        x = p_ref[:, pl.ds(pl.multiple_of(b * TILE, TILE), TILE)]
        t_ref[b] = dot(inner_ref[...], jnp.concatenate([x] * 3, axis=1), NT)

    @pl.loop(0, tiles, unroll=tiles)
    def _(g):
        at = pl.ds(pl.multiple_of(g * 16, 16), 16)
        x = t_ref[:, at, :].reshape(TILE, ROWS)
        high = x.astype(jnp.bfloat16)
        low = (x - high.astype(jnp.float32)).astype(jnp.bfloat16)
        left = jnp.concatenate([outer_ref[:, : 2 * TILE], outer_ref[:, :TILE]], axis=1)
        y = dot(left, jnp.concatenate([high, high, low], axis=0), NN)
        t_ref[:, at, :] = y.reshape(16, 16, ROWS)

    @pl.loop(0, tiles, unroll=tiles)
    def _(b):
        y = dot(order_ref[...], t_ref[b].astype(jnp.bfloat16), NN)
        w_ref[pl.ds(pl.multiple_of(b * TILE, TILE), TILE), :] = y.astype(jnp.bfloat16)


def weigh(rows, tiles, copied=False):
    width = rows.shape[1]
    out = jax.ShapeDtypeStruct((width, ROWS), jnp.bfloat16)
    return pl.pallas_call(
        weigh_kernel,
        out_shape=(out, jax.ShapeDtypeStruct(rows.shape, rows.dtype)) if copied else out,
        scratch_shapes=[pltpu.VMEM((width // TILE, TILE, ROWS), jnp.float32)],
        compiler_params=pltpu.CompilerParams(vmem_limit_bytes=24 * 2**20),
        cost_estimate=COST,
    )(rows, *tiles)


def products_kernel(picks, n_p, n_w, place_ref, *refs):
    p_refs, w_refs = refs[:n_p], refs[n_p : n_p + n_w]
    out_ref, total = refs[-2:]

    def score(slot, p, w):
        total[slot] = dot(p_refs[p][...], w_refs[w][...], NN)

    for slot, (axis, least, below, reached) in enumerate(picks):
        if axis is None:
            score(slot, *reached)
        else:
            here = place_ref[axis]
            pl.when(here < least)(functools.partial(score, slot, *below))
            pl.when(here >= least)(functools.partial(score, slot, *reached))
    end = len(picks) * PIECE
    left = out_ref.shape[2] - end
    top = jnp.max(jnp.abs(total[...]))
    out_ref[:, :, end:] = jnp.full((NC, NL, left, LANES), top, jnp.float32)
    for pair in range(len(picks) // 2):
        a, b = total[2 * pair], total[2 * pair + 1]
        rest = jnp.concatenate([a[:, LANES:], b[:, LANES:]], axis=1)
        for n, piece in enumerate((a[:, :LANES], b[:, :LANES], rest)):
            to = (3 * pair + n) * OWN
            for chip in range(NL):
                for core in range(NC):
                    at = (chip * NC + core) * OWN
                    out_ref[core, chip, to : to + OWN] = piece[at : at + OWN]


def products(plains, weights, picks):
    place = jnp.stack([lax.axis_index("zl"), lax.axis_index("x")]).astype(jnp.int32)
    vmem = pl.BlockSpec(memory_space=pltpu.VMEM)
    height = (len(picks) * PIECE // 8 + 1) * 8
    return pl.pallas_call(
        functools.partial(products_kernel, picks, len(plains), len(weights)),
        out_shape=jax.ShapeDtypeStruct((NC, NL, height, LANES), jnp.float32),
        in_specs=[pl.BlockSpec(memory_space=pltpu.SMEM)] + [vmem] * (len(plains) + len(weights)),
        out_specs=vmem,
        scratch_shapes=[pltpu.VMEM((len(picks), ROWS, ROWS), jnp.float32)],
        compiler_params=pltpu.CompilerParams(vmem_limit_bytes=24 * 2**20),
        cost_estimate=COST,
    )(place, *plains, *weights)


def unpacked(part, slots):
    part = part[: slots * PIECE].reshape(slots // 2, 3, OWN, LANES)
    rest = part[:, 2].reshape(slots // 2, OWN, 2, ROWS - LANES).transpose(0, 2, 1, 3)
    return jnp.concatenate([part[:, :2], rest], axis=-1).reshape(slots, OWN, ROWS)


def core_sum(sums, slots):
    pair = lax.all_to_all(sums, "c", 0, 0, tiled=False)
    end = slots * PIECE
    bound = jnp.maximum(pair[0, :, end:] + pair[1, :, end:], 1e-30)
    power = jnp.floor(jnp.log2(bound)) - 14
    scaled = (pair[0, :, :end] + pair[1, :, :end]) * jnp.exp2(-power[:, :1])
    return jnp.concatenate([scaled, power], axis=1).astype(jnp.float16)


def chip_sum(got, slots):
    end = slots * PIECE
    got = got.astype(jnp.float32)
    return unpacked((got[:, :end] * jnp.exp2(got[:, end : end + 1])).sum(0), slots)


def turned(value, steps):
    return lax.dynamic_slice_in_dim(jnp.concatenate([value, value]), steps, value.shape[0])


def per_device(grads, in_factor, out_factor):
    factor = 1.0 / math.sqrt(NL * NC * grads.shape[-1])
    z, x = lax.axis_index("zl"), lax.axis_index("x")
    tiles = factor_tiles(in_factor[0], out_factor[0])
    half = ROWS // 2
    p0 = grads[0]
    p1, p3 = moved(p0, "x", 1), moved(p0, "x", -1)
    p4 = lax.ppermute(p0, "zl", [(0, 2), (3, 1), (1, 0)])
    w0, own = weigh(p0, tiles, copied=True)
    p5 = lax.ppermute(own, "zl", [(0, 3), (2, 1), (3, 2)])
    p2 = jnp.concatenate([moved(p1[:half], "x", 1), moved(p3[half:], "x", -1)])
    w1, w2, w3, w4 = (weigh(p, tiles) for p in (p1, p2, p3, p4))
    early = products(
        [own, p1, p2, p3, p4],
        [w0, w1, w2, w3, w4],
        [
            (None, 0, None, (0, 0)),
            (1, 1, (1, 0), (0, 1)),
            (None, 0, None, (0, 2)),
            (None, 0, None, (4, 0)),
            (1, 1, (4, 1), (1, 4)),
            (1, 2, (4, 2), (2, 4)),
            (1, 3, (4, 3), (3, 4)),
            (None, 0, None, (0, 4)),
        ],
    )
    late = products([p4, p5], [w0, w1, w2, w3], [(0, 1, (0, r), (1, r)) for r in range(NX)])
    early, late = core_sum(early, 8), core_sum(late, 4)
    got = lax.all_to_all(
        jnp.concatenate([early, late], axis=1), ("y", "zh"), 0, 0, tiled=False
    )
    slots = chip_sum(got[:, : early.shape[1]], 8)
    row, two, again = slots[:3], slots[3:7], slots[7]
    following = chip_sum(got[:, early.shape[1] :], 4)
    out = [None] * 9
    out[0], out[4] = row[0], following[0]
    across = lax.ppermute(
        jnp.concatenate([again[None], two[1:]]), "zl", [(1, 3), (2, 0)]
    )
    middle = (z == 1) | (z == 2)
    out[8] = jnp.where(middle, two[0], across[0])
    other = [two[0]] + [jnp.where(x >= r, row[min(r, 2)], two[r]) for r in range(1, NX)]
    sent = jnp.stack([following, jnp.stack(other)], axis=1)[::-1]
    got = lax.all_to_all(turned(sent, (NX - 1 - x) % NX), "x", 0, 0, tiled=False)
    got = turned(got, x)
    for r in range(1, NX):
        back = got[r]
        inside = x + r < NX
        near = row[1] if r == 3 else back[1]
        far = jnp.where(middle, back[1], across[NX - r])
        out[r] = jnp.where(inside, near, back[0])
        out[r + 4] = jnp.where(inside, back[0], far)
    return (jnp.stack(out) * factor).transpose(2, 0, 1)


def solution(mesh):
    fine = Mesh(mesh.devices.reshape(NZ, NX, NY, NH, NC), ("zl", "x", "y", "zh", "c"))
    layer, group = ("y", "zh", "c"), ("zl", "x")
    in_specs = (P(layer, group, None), P(layer, None, None), P(layer, None, None))
    return jax.shard_map(
        per_device, mesh=fine, in_specs=in_specs, out_specs=P(group, None, layer), check_vma=False
    )
```

```python
import functools
import math

import jax
import jax.numpy as jnp
import numpy as np
from jax import lax
from jax.experimental import pallas as pl
from jax.experimental.pallas import tpu as pltpu
from jax.sharding import Mesh, PartitionSpec as P

NZ, NX, NY, NH, NC = 4, 4, 8, 2, 2
NL = NY * NH
ROWS = 192
OWN = ROWS // (NL * NC)
LANES = 128
PIECE = OWN * ROWS // LANES
GROUP = 40
TILE = 256
NN, NT = ((1,), (0,)), ((1,), (1,))
COST = pl.CostEstimate(flops=10**10, bytes_accessed=10**6, transcendentals=0)


def moved(value, axis, steps):
    count = lax.axis_size(axis)
    return lax.ppermute(value, axis, [(s, (s + steps) % count) for s in range(count)])


def spread():
    at = np.arange(TILE)
    six = np.arange(64)
    by_four = (at[:, None] // 4 == six).astype(np.float32)
    by_last = (at[:, None] % 64 == six).astype(np.float32)
    mixed = (at[:, None] // 16 * 4 + at[:, None] % 4 == six).astype(np.float32)
    inner = (at[:, None] % 4 == at // 64).astype(np.float32)
    outer = (at[:, None] // 4 % 4 == at // 4 % 4).astype(np.float32)
    order = np.zeros((TILE, TILE), np.float32)
    order[at, at % 64 * 4 + at // 64] = 1
    return [jnp.asarray(m) for m in (by_four, by_last, mixed, inner, outer)], jnp.asarray(
        order, jnp.bfloat16
    )


def tiles_kernel(in_ref, out_ref, four_ref, last_ref, mixed_ref, im_ref, om_ref, a_ref, b_ref):
    def exact(a, b, dims):
        return lax.dot_general(
            a,
            b,
            (dims, ((), ())),
            precision=lax.Precision.HIGHEST,
            preferred_element_type=jnp.float32,
        )

    def parts(ref, matrix):
        for part in range(3):
            rounded = matrix.astype(jnp.bfloat16)
            ref[:, part * TILE : (part + 1) * TILE] = rounded
            matrix = matrix - rounded.astype(jnp.float32)

    inner = exact(exact(four_ref[...], in_ref[...], NT), last_ref[...], NT)
    parts(a_ref, inner * im_ref[...])
    outer = exact(exact(mixed_ref[...], out_ref[...], NN), mixed_ref[...], NT)
    parts(b_ref, outer * om_ref[...])


def factor_tiles(in_mat, out_mat):
    matrices, order = spread()
    shape = jax.ShapeDtypeStruct((TILE, 3 * TILE), jnp.bfloat16)
    inner, outer = pl.pallas_call(
        tiles_kernel, out_shape=(shape, shape), cost_estimate=COST
    )(in_mat, out_mat, *matrices)
    return inner, outer, order


def dot(a, b, dims):
    return lax.dot_general(a, b, (dims, ((), ())), preferred_element_type=jnp.float32)


def weigh_kernel(p_ref, inner_ref, outer_ref, order_ref, w_ref, *rest):
    *copies, t_ref = rest
    tiles = p_ref.shape[1] // TILE
    for copy in copies:
        copy[...] = p_ref[...]

    @pl.loop(0, tiles, unroll=tiles)
    def _(b):
        x = p_ref[:, pl.ds(pl.multiple_of(b * TILE, TILE), TILE)]
        t_ref[b] = dot(inner_ref[...], jnp.concatenate([x] * 3, axis=1), NT)

    @pl.loop(0, tiles, unroll=tiles)
    def _(g):
        at = pl.ds(pl.multiple_of(g * 16, 16), 16)
        x = t_ref[:, at, :].reshape(TILE, ROWS)
        high = x.astype(jnp.bfloat16)
        low = (x - high.astype(jnp.float32)).astype(jnp.bfloat16)
        left = jnp.concatenate([outer_ref[:, : 2 * TILE], outer_ref[:, :TILE]], axis=1)
        y = dot(left, jnp.concatenate([high, high, low], axis=0), NN)
        t_ref[:, at, :] = y.reshape(16, 16, ROWS)

    @pl.loop(0, tiles, unroll=tiles)
    def _(b):
        y = dot(order_ref[...], t_ref[b].astype(jnp.bfloat16), NN)
        w_ref[pl.ds(pl.multiple_of(b * TILE, TILE), TILE), :] = y.astype(jnp.bfloat16)


def weigh(rows, tiles, copied=False):
    width = rows.shape[1]
    out = jax.ShapeDtypeStruct((width, ROWS), jnp.bfloat16)
    return pl.pallas_call(
        weigh_kernel,
        out_shape=(out, jax.ShapeDtypeStruct(rows.shape, rows.dtype)) if copied else out,
        scratch_shapes=[pltpu.VMEM((width // TILE, TILE, ROWS), jnp.float32)],
        compiler_params=pltpu.CompilerParams(vmem_limit_bytes=24 * 2**20),
        cost_estimate=COST,
    )(rows, *tiles)


def products_kernel(picks, groups, n_p, n_w, place_ref, *refs):
    p_refs, w_refs = refs[:n_p], refs[n_p : n_p + n_w]
    out_ref, total = refs[-2:]

    def score(slot, p, w):
        total[slot] = dot(p_refs[p][...], w_refs[w][...], NN)

    for slot, (axis, least, below, reached) in enumerate(picks):
        if axis is None:
            score(slot, *reached)
        else:
            here = place_ref[axis]
            pl.when(here < least)(functools.partial(score, slot, *below))
            pl.when(here >= least)(functools.partial(score, slot, *reached))
    top = jnp.full((NC, NL, GROUP - 4 * PIECE, LANES), jnp.max(jnp.abs(total[...])), jnp.float32)
    for group, slots in enumerate(groups):
        start = group * GROUP
        out_ref[:, :, start + 4 * PIECE : start + GROUP] = top
        for pair in range(2):
            a, b = total[slots[2 * pair]], total[slots[2 * pair + 1]]
            rest = jnp.concatenate([a[:, LANES:], b[:, LANES:]], axis=1)
            for n, piece in enumerate((a[:, :LANES], b[:, :LANES], rest)):
                to = start + (3 * pair + n) * OWN
                for chip in range(NL):
                    for core in range(NC):
                        at = (chip * NC + core) * OWN
                        out_ref[core, chip, to : to + OWN] = piece[at : at + OWN]


def products(plains, weights, picks, groups):
    place = jnp.stack([lax.axis_index("zl"), lax.axis_index("x")]).astype(jnp.int32)
    vmem = pl.BlockSpec(memory_space=pltpu.VMEM)
    height = len(groups) * GROUP
    return pl.pallas_call(
        functools.partial(products_kernel, picks, groups, len(plains), len(weights)),
        out_shape=jax.ShapeDtypeStruct((NC, NL, height, LANES), jnp.float32),
        in_specs=[pl.BlockSpec(memory_space=pltpu.SMEM)] + [vmem] * (len(plains) + len(weights)),
        out_specs=vmem,
        scratch_shapes=[pltpu.VMEM((len(picks), ROWS, ROWS), jnp.float32)],
        compiler_params=pltpu.CompilerParams(vmem_limit_bytes=24 * 2**20),
        cost_estimate=COST,
    )(place, *plains, *weights)


def core_sum(sums):
    pair = lax.all_to_all(sums, "c", 0, 0, tiled=False)
    pair = pair.reshape(NC, NL, -1, GROUP, LANES)
    end = 4 * PIECE
    bound = jnp.maximum(pair[0, :, :, end:] + pair[1, :, :, end:], 1e-30)
    power = jnp.floor(jnp.log2(bound)) - 14
    scaled = (pair[0, :, :, :end] + pair[1, :, :, :end]) * jnp.exp2(-power[:, :, :1])
    return jnp.concatenate([scaled, power], axis=2).astype(jnp.float16)


def chip_sum(sums):
    n = sums.shape[1]
    got = lax.all_to_all(sums.reshape(NY, NH * n * GROUP, LANES), "y", 0, 0, tiled=False)
    got = got.astype(jnp.float32).reshape(NY, NH, n, GROUP, LANES)
    end = 4 * PIECE
    part = (got[..., :end, :] * jnp.exp2(got[..., end : end + 1, :])).sum(0)
    part = part.reshape(NH, n, 2, 3, OWN, LANES)
    rest = part[..., 2, :, :].reshape(NH, n, 2, OWN, 2, ROWS - LANES).swapaxes(3, 4)
    return jnp.concatenate([part[..., :2, :, :], rest], axis=-1).reshape(NH, n, 4, OWN, ROWS)


def turned(value, steps):
    return lax.dynamic_slice_in_dim(jnp.concatenate([value, value]), steps, value.shape[0])


def per_device(grads, in_factor, out_factor):
    factor = 1.0 / math.sqrt(NL * NC * grads.shape[-1])
    z, x = lax.axis_index("zl"), lax.axis_index("x")
    tiles = factor_tiles(in_factor[0], out_factor[0])
    half = ROWS // 2
    p0 = grads[0]
    p1, p3 = moved(p0, "x", 1), moved(p0, "x", -1)
    p4 = lax.ppermute(p0, "zl", [(0, 2), (3, 1), (1, 0)])
    w0, own = weigh(p0, tiles, copied=True)
    p5 = lax.ppermute(own, "zl", [(0, 3), (2, 1), (3, 2)])
    p2 = jnp.concatenate([moved(p1[:half], "x", 1), moved(p3[half:], "x", -1)])
    w1, w2, w3, w4 = (weigh(p, tiles) for p in (p1, p2, p3, p4))
    early = products(
        [own, p1, p2, p3, p4],
        [w0, w1, w2, w3, w4],
        [
            (None, 0, None, (0, 0)),
            (1, 1, (1, 0), (0, 1)),
            (None, 0, None, (0, 2)),
            (None, 0, None, (4, 0)),
            (1, 1, (4, 1), (1, 4)),
            (1, 2, (4, 2), (2, 4)),
            (1, 3, (4, 3), (3, 4)),
            (None, 0, None, (0, 4)),
        ],
        [(0, 1, 2, 2), (3, 4, 5, 6), (7, 4, 5, 6)],
    )
    late = products(
        [p4, p5],
        [w0, w1, w2, w3],
        [(0, 1, (0, r), (1, r)) for r in range(NX)],
        [tuple(range(NX))],
    )
    early = core_sum(early)
    across = lax.ppermute(early[:, 2], "zl", [(1, 3), (2, 0)])
    middle = (z == 1) | (z == 2)
    two = jnp.where(middle, early[:, 1], across)
    sums = jnp.concatenate([early[:, :1], two[:, None], core_sum(late)], axis=1)
    sums = chip_sum(sums)
    row, two, following = sums[:, 0], sums[:, 1], sums[:, 2]
    own = [row[:, 0], jnp.where(x == 0, row[:, 1], two[:, 1]), two[:, 2], two[:, 3]]
    sent = [
        jnp.stack(
            [
                following[:, r],
                jnp.where(x >= r, row[:, min(r, 2)], two[:, r]) if r else two[:, 0],
                *own,
            ],
            axis=1,
        )
        for r in reversed(range(NX))
    ]
    sent = turned(jnp.stack(sent), (NX - 1 - x) % NX)
    got = lax.all_to_all(
        sent.reshape(NX * NH, 6 * OWN, ROWS), ("x", "zh"), 0, 0, tiled=False
    )
    got = turned(got.reshape(NX, NH, 6, OWN, ROWS).sum(1), x)
    out = [None] * 9
    out[4], out[8], out[0] = got[0, 0], got[0, 1], got[0, 2]
    for r in range(1, NX):
        inside = x + r < NX
        near = got[0, 3] if r == 3 else got[r, 1]
        far = jnp.where(middle, got[r, 1], got[0, 6 - r])
        out[r] = jnp.where(inside, near, got[r, 0])
        out[r + 4] = jnp.where(inside, got[r, 0], far)
    return (jnp.stack(out) * factor).transpose(2, 0, 1)


def solution(mesh):
    fine = Mesh(mesh.devices.reshape(NZ, NX, NY, NH, NC), ("zl", "x", "y", "zh", "c"))
    layer, group = ("y", "zh", "c"), ("zl", "x")
    in_specs = (P(layer, group, None), P(layer, None, None), P(layer, None, None))
    return jax.shard_map(
        per_device, mesh=fine, in_specs=in_specs, out_specs=P(group, None, layer), check_vma=False
    )
```

```python
import functools
import math

import jax
import jax.numpy as jnp
import numpy as np
from jax import lax
from jax.experimental import pallas as pl
from jax.experimental.pallas import tpu as pltpu
from jax.sharding import Mesh, PartitionSpec as P

NZ, NX, NY, NH, NC = 4, 4, 8, 2, 2
NL = NY * NH
ROWS = 192
OWN = ROWS // (NL * NC)
LANES = 128
PIECE = OWN * ROWS // LANES
GROUP = 40
TILE = 256
NN, NT = ((1,), (0,)), ((1,), (1,))
COST = pl.CostEstimate(flops=10**10, bytes_accessed=10**6, transcendentals=0)


def moved(value, axis, steps):
    count = lax.axis_size(axis)
    return lax.ppermute(value, axis, [(s, (s + steps) % count) for s in range(count)])


def spread():
    at = np.arange(TILE)
    six = np.arange(64)
    by_four = (at[:, None] // 4 == six).astype(np.float32)
    by_last = (at[:, None] % 64 == six).astype(np.float32)
    mixed = (at[:, None] // 16 * 4 + at[:, None] % 4 == six).astype(np.float32)
    inner = (at[:, None] % 4 == at // 64).astype(np.float32)
    outer = (at[:, None] // 4 % 4 == at // 4 % 4).astype(np.float32)
    order = np.zeros((TILE, TILE), np.float32)
    order[at, at % 64 * 4 + at // 64] = 1
    return [jnp.asarray(m) for m in (by_four, by_last, mixed, inner, outer)], jnp.asarray(
        order, jnp.bfloat16
    )


def tiles_kernel(in_ref, out_ref, four_ref, last_ref, mixed_ref, im_ref, om_ref, a_ref, b_ref):
    def exact(a, b, dims):
        return lax.dot_general(
            a,
            b,
            (dims, ((), ())),
            precision=lax.Precision.HIGHEST,
            preferred_element_type=jnp.float32,
        )

    def parts(ref, matrix):
        for part in range(3):
            rounded = matrix.astype(jnp.bfloat16)
            ref[:, part * TILE : (part + 1) * TILE] = rounded
            matrix = matrix - rounded.astype(jnp.float32)

    inner = exact(exact(four_ref[...], in_ref[...], NT), last_ref[...], NT)
    parts(a_ref, inner * im_ref[...])
    outer = exact(exact(mixed_ref[...], out_ref[...], NN), mixed_ref[...], NT)
    parts(b_ref, outer * om_ref[...])


def factor_tiles(in_mat, out_mat):
    matrices, order = spread()
    shape = jax.ShapeDtypeStruct((TILE, 3 * TILE), jnp.bfloat16)
    inner, outer = pl.pallas_call(
        tiles_kernel, out_shape=(shape, shape), cost_estimate=COST
    )(in_mat, out_mat, *matrices)
    return inner, outer, order


def dot(a, b, dims):
    return lax.dot_general(a, b, (dims, ((), ())), preferred_element_type=jnp.float32)


def weigh_kernel(p_ref, inner_ref, outer_ref, order_ref, w_ref, *rest):
    *copies, t_ref = rest
    tiles = p_ref.shape[1] // TILE
    for copy in copies:
        copy[...] = p_ref[...]

    @pl.loop(0, tiles, unroll=tiles)
    def _(b):
        x = p_ref[:, pl.ds(pl.multiple_of(b * TILE, TILE), TILE)]
        t_ref[b] = dot(inner_ref[...], jnp.concatenate([x] * 3, axis=1), NT)

    @pl.loop(0, tiles, unroll=tiles)
    def _(g):
        at = pl.ds(pl.multiple_of(g * 16, 16), 16)
        x = t_ref[:, at, :].reshape(TILE, ROWS)
        high = x.astype(jnp.bfloat16)
        low = (x - high.astype(jnp.float32)).astype(jnp.bfloat16)
        left = jnp.concatenate([outer_ref[:, : 2 * TILE], outer_ref[:, :TILE]], axis=1)
        y = dot(left, jnp.concatenate([high, high, low], axis=0), NN)
        t_ref[:, at, :] = y.reshape(16, 16, ROWS)

    @pl.loop(0, tiles, unroll=tiles)
    def _(b):
        y = dot(order_ref[...], t_ref[b].astype(jnp.bfloat16), NN)
        w_ref[pl.ds(pl.multiple_of(b * TILE, TILE), TILE), :] = y.astype(jnp.bfloat16)


def weigh(rows, tiles, copied=False):
    width = rows.shape[1]
    out = jax.ShapeDtypeStruct((width, ROWS), jnp.bfloat16)
    return pl.pallas_call(
        weigh_kernel,
        out_shape=(out, jax.ShapeDtypeStruct(rows.shape, rows.dtype)) if copied else out,
        scratch_shapes=[pltpu.VMEM((width // TILE, TILE, ROWS), jnp.float32)],
        compiler_params=pltpu.CompilerParams(vmem_limit_bytes=24 * 2**20),
        cost_estimate=COST,
    )(rows, *tiles)


def products_kernel(picks, groups, n_p, n_w, place_ref, *refs):
    p_refs, w_refs = refs[:n_p], refs[n_p : n_p + n_w]
    out_ref, total = refs[-2:]

    def score(slot, p, w):
        total[slot] = dot(p_refs[p][...], w_refs[w][...], NN)

    for slot, (axis, least, below, reached) in enumerate(picks):
        if axis is None:
            score(slot, *reached)
        else:
            here = place_ref[axis]
            pl.when(here < least)(functools.partial(score, slot, *below))
            pl.when(here >= least)(functools.partial(score, slot, *reached))
    top = jnp.full((NC, NL, GROUP - 4 * PIECE, LANES), jnp.max(jnp.abs(total[...])), jnp.float32)
    for group, slots in enumerate(groups):
        start = group * GROUP
        out_ref[:, :, start + 4 * PIECE : start + GROUP] = top
        for pair in range(2):
            a, b = total[slots[2 * pair]], total[slots[2 * pair + 1]]
            rest = jnp.concatenate([a[:, LANES:], b[:, LANES:]], axis=1)
            for n, piece in enumerate((a[:, :LANES], b[:, :LANES], rest)):
                to = start + (3 * pair + n) * OWN
                for chip in range(NL):
                    for core in range(NC):
                        at = (chip * NC + core) * OWN
                        out_ref[core, chip, to : to + OWN] = piece[at : at + OWN]


def products(plains, weights, picks, groups):
    place = jnp.stack([lax.axis_index("zl"), lax.axis_index("x")]).astype(jnp.int32)
    vmem = pl.BlockSpec(memory_space=pltpu.VMEM)
    height = len(groups) * GROUP
    return pl.pallas_call(
        functools.partial(products_kernel, picks, groups, len(plains), len(weights)),
        out_shape=jax.ShapeDtypeStruct((NC, NL, height, LANES), jnp.float32),
        in_specs=[pl.BlockSpec(memory_space=pltpu.SMEM)] + [vmem] * (len(plains) + len(weights)),
        out_specs=vmem,
        scratch_shapes=[pltpu.VMEM((len(picks), ROWS, ROWS), jnp.float32)],
        compiler_params=pltpu.CompilerParams(vmem_limit_bytes=24 * 2**20),
        cost_estimate=COST,
    )(place, *plains, *weights)


def core_sum(sums):
    pair = lax.all_to_all(sums, "c", 0, 0, tiled=False)
    pair = pair.reshape(NC, NL, -1, GROUP, LANES)
    end = 4 * PIECE
    bound = jnp.maximum(pair[0, :, :, end:] + pair[1, :, :, end:], 1e-30)
    power = jnp.floor(jnp.log2(bound)) - 14
    scaled = (pair[0, :, :, :end] + pair[1, :, :, :end]) * jnp.exp2(-power[:, :, :1])
    return jnp.concatenate([scaled, power], axis=2).astype(jnp.float16)


def chip_sum(sums):
    n = sums.shape[1]
    sums = sums.reshape(NL, n * GROUP, LANES)
    got = lax.all_to_all(sums, ("y", "zh"), 0, 0, tiled=False)
    got = got.astype(jnp.float32).reshape(NL, n, GROUP, LANES)
    end = 4 * PIECE
    part = (got[..., :end, :] * jnp.exp2(got[..., end : end + 1, :])).sum(0)
    part = part.reshape(n, 2, 3, OWN, LANES)
    rest = part[:, :, 2].reshape(n, 2, OWN, 2, ROWS - LANES).swapaxes(2, 3)
    return jnp.concatenate([part[:, :, :2], rest], axis=-1).reshape(n, 4, OWN, ROWS)


def turned(value, steps):
    return lax.dynamic_slice_in_dim(jnp.concatenate([value, value]), steps, value.shape[0])


def per_device(grads, in_factor, out_factor):
    factor = 1.0 / math.sqrt(NL * NC * grads.shape[-1])
    z, x = lax.axis_index("zl"), lax.axis_index("x")
    tiles = factor_tiles(in_factor[0], out_factor[0])
    half = ROWS // 2
    p0 = grads[0]
    p1, p3 = moved(p0, "x", 1), moved(p0, "x", -1)
    p4 = lax.ppermute(p0, "zl", [(0, 2), (3, 1), (1, 0)])
    w0, own = weigh(p0, tiles, copied=True)
    p5 = lax.ppermute(own, "zl", [(0, 3), (2, 1), (3, 2)])
    p2 = jnp.concatenate([moved(p1[:half], "x", 1), moved(p3[half:], "x", -1)])
    w1, w2, w3, w4 = (weigh(p, tiles) for p in (p1, p2, p3, p4))
    early = products(
        [own, p1, p2, p3, p4],
        [w0, w1, w2, w3, w4],
        [
            (None, 0, None, (0, 0)),
            (1, 1, (1, 0), (0, 1)),
            (None, 0, None, (0, 2)),
            (None, 0, None, (4, 0)),
            (1, 1, (4, 1), (1, 4)),
            (1, 2, (4, 2), (2, 4)),
            (1, 3, (4, 3), (3, 4)),
            (None, 0, None, (0, 4)),
        ],
        [(0, 1, 2, 2), (3, 4, 5, 6), (7, 4, 5, 6)],
    )
    late = products(
        [p4, p5],
        [w0, w1, w2, w3],
        [(0, 1, (0, r), (1, r)) for r in range(NX)],
        [tuple(range(NX))],
    )
    early = core_sum(early)
    across = lax.ppermute(early[:, 2], "zl", [(1, 3), (2, 0)])
    middle = (z == 1) | (z == 2)
    two = jnp.where(middle, early[:, 1], across)
    sums = jnp.concatenate([early[:, :1], two[:, None], core_sum(late)], axis=1)
    row, two, following = chip_sum(sums)
    other = [two[0]] + [jnp.where(x >= r, row[min(r, 2)], two[r]) for r in range(1, NX)]
    sent = turned(jnp.stack([following, jnp.stack(other)], axis=1)[::-1], (NX - 1 - x) % NX)
    got = turned(lax.all_to_all(sent, "x", 0, 0, tiled=False), x)
    out = [None] * 9
    out[0], out[4], out[8] = row[0], following[0], two[0]
    for r in range(1, NX):
        inside = x + r < NX
        near = row[1] if r == 3 else got[r, 1]
        far = jnp.where(middle, got[r, 1], two[NX - r])
        out[r] = jnp.where(inside, near, got[r, 0])
        out[r + 4] = jnp.where(inside, got[r, 0], far)
    return (jnp.stack(out) * factor).transpose(2, 0, 1)


def solution(mesh):
    fine = Mesh(mesh.devices.reshape(NZ, NX, NY, NH, NC), ("zl", "x", "y", "zh", "c"))
    layer, group = ("y", "zh", "c"), ("zl", "x")
    in_specs = (P(layer, group, None), P(layer, None, None), P(layer, None, None))
    return jax.shard_map(
        per_device, mesh=fine, in_specs=in_specs, out_specs=P(group, None, layer), check_vma=False
    )
```

```python
import functools
import math

import jax
import jax.numpy as jnp
import numpy as np
from jax import lax
from jax.experimental import pallas as pl
from jax.experimental.pallas import tpu as pltpu
from jax.sharding import Mesh, PartitionSpec as P

NZ, NX, NY, NH, NC = 4, 4, 8, 2, 2
NL = NY * NH
ROWS = 192
OWN = ROWS // (NL * NC)
LANES = 128
PIECE = OWN * ROWS // LANES
GROUP = 40
TILE = 256
NN, NT = ((1,), (0,)), ((1,), (1,))
COST = pl.CostEstimate(flops=10**10, bytes_accessed=10**6, transcendentals=0)


def moved(value, axis, steps):
    count = lax.axis_size(axis)
    return lax.ppermute(value, axis, [(s, (s + steps) % count) for s in range(count)])


def spread():
    at = np.arange(TILE)
    six = np.arange(64)
    by_four = (at[:, None] // 4 == six).astype(np.float32)
    by_last = (at[:, None] % 64 == six).astype(np.float32)
    mixed = (at[:, None] // 16 * 4 + at[:, None] % 4 == six).astype(np.float32)
    inner = (at[:, None] % 4 == at // 64).astype(np.float32)
    outer = (at[:, None] // 4 % 4 == at // 4 % 4).astype(np.float32)
    order = np.zeros((TILE, TILE), np.float32)
    order[at, at % 64 * 4 + at // 64] = 1
    return [jnp.asarray(m) for m in (by_four, by_last, mixed, inner, outer)], jnp.asarray(
        order, jnp.bfloat16
    )


def tiles_kernel(in_ref, out_ref, four_ref, last_ref, mixed_ref, im_ref, om_ref, a_ref, b_ref):
    def exact(a, b, dims):
        return lax.dot_general(
            a,
            b,
            (dims, ((), ())),
            precision=lax.Precision.HIGHEST,
            preferred_element_type=jnp.float32,
        )

    def parts(ref, matrix):
        for part in range(3):
            rounded = matrix.astype(jnp.bfloat16)
            ref[:, part * TILE : (part + 1) * TILE] = rounded
            matrix = matrix - rounded.astype(jnp.float32)

    inner = exact(exact(four_ref[...], in_ref[...], NT), last_ref[...], NT)
    parts(a_ref, inner * im_ref[...])
    outer = exact(exact(mixed_ref[...], out_ref[...], NN), mixed_ref[...], NT)
    parts(b_ref, outer * om_ref[...])


def factor_tiles(in_mat, out_mat):
    matrices, order = spread()
    shape = jax.ShapeDtypeStruct((TILE, 3 * TILE), jnp.bfloat16)
    inner, outer = pl.pallas_call(
        tiles_kernel, out_shape=(shape, shape), cost_estimate=COST
    )(in_mat, out_mat, *matrices)
    return inner, outer, order


def dot(a, b, dims):
    return lax.dot_general(a, b, (dims, ((), ())), preferred_element_type=jnp.float32)


def weigh_kernel(p_ref, inner_ref, outer_ref, order_ref, w_ref, *rest):
    *copies, t_ref = rest
    tiles = p_ref.shape[1] // TILE
    for copy in copies:
        copy[...] = p_ref[...]

    @pl.loop(0, tiles, unroll=tiles)
    def _(b):
        x = p_ref[:, pl.ds(pl.multiple_of(b * TILE, TILE), TILE)]
        t_ref[b] = dot(inner_ref[...], jnp.concatenate([x] * 3, axis=1), NT)

    @pl.loop(0, tiles, unroll=tiles)
    def _(g):
        at = pl.ds(pl.multiple_of(g * 16, 16), 16)
        x = t_ref[:, at, :].reshape(TILE, ROWS)
        high = x.astype(jnp.bfloat16)
        low = (x - high.astype(jnp.float32)).astype(jnp.bfloat16)
        left = jnp.concatenate([outer_ref[:, : 2 * TILE], outer_ref[:, :TILE]], axis=1)
        y = dot(left, jnp.concatenate([high, high, low], axis=0), NN)
        t_ref[:, at, :] = y.reshape(16, 16, ROWS)

    @pl.loop(0, tiles, unroll=tiles)
    def _(b):
        y = dot(order_ref[...], t_ref[b].astype(jnp.bfloat16), NN)
        w_ref[pl.ds(pl.multiple_of(b * TILE, TILE), TILE), :] = y.astype(jnp.bfloat16)


def weigh(rows, tiles, copied=False):
    width = rows.shape[1]
    out = jax.ShapeDtypeStruct((width, ROWS), jnp.bfloat16)
    return pl.pallas_call(
        weigh_kernel,
        out_shape=(out, jax.ShapeDtypeStruct(rows.shape, rows.dtype)) if copied else out,
        scratch_shapes=[pltpu.VMEM((width // TILE, TILE, ROWS), jnp.float32)],
        compiler_params=pltpu.CompilerParams(vmem_limit_bytes=24 * 2**20),
        cost_estimate=COST,
    )(rows, *tiles)


def products_kernel(picks, groups, n_p, n_w, place_ref, *refs):
    p_refs, w_refs = refs[:n_p], refs[n_p : n_p + n_w]
    given, (out_ref, total) = refs[n_p + n_w : -2], refs[-2:]
    first = 0
    if given:
        first = given[0].shape[2]
        out_ref[:, :, :first] = given[0][...]

    def score(slot, p, w):
        total[slot] = dot(p_refs[p][...], w_refs[w][...], NN)

    for slot, (axis, least, below, reached) in enumerate(picks):
        if axis is None:
            score(slot, *reached)
        else:
            here = place_ref[axis]
            pl.when(here < least)(functools.partial(score, slot, *below))
            pl.when(here >= least)(functools.partial(score, slot, *reached))
    top = jnp.full((NC, NL, GROUP - 4 * PIECE, LANES), jnp.max(jnp.abs(total[...])), jnp.float32)
    for group, slots in enumerate(groups):
        start = first + group * GROUP
        out_ref[:, :, start + 4 * PIECE : start + GROUP] = top
        for pair in range(2):
            a, b = total[slots[2 * pair]], total[slots[2 * pair + 1]]
            rest = jnp.concatenate([a[:, LANES:], b[:, LANES:]], axis=1)
            for n, piece in enumerate((a[:, :LANES], b[:, :LANES], rest)):
                to = start + (3 * pair + n) * OWN
                for chip in range(NL):
                    for core in range(NC):
                        at = (chip * NC + core) * OWN
                        out_ref[core, chip, to : to + OWN] = piece[at : at + OWN]


def products(plains, weights, picks, groups, sums=None):
    place = jnp.stack([lax.axis_index("zl"), lax.axis_index("x")]).astype(jnp.int32)
    vmem = pl.BlockSpec(memory_space=pltpu.VMEM)
    given = () if sums is None else (sums,)
    height = sum(v.shape[2] for v in given) + len(groups) * GROUP
    return pl.pallas_call(
        functools.partial(products_kernel, picks, groups, len(plains), len(weights)),
        out_shape=jax.ShapeDtypeStruct((NC, NL, height, LANES), jnp.float32),
        in_specs=[pl.BlockSpec(memory_space=pltpu.SMEM)] + [vmem] * (len(plains) + len(weights) + len(given)),
        out_specs=vmem,
        scratch_shapes=[pltpu.VMEM((len(picks), ROWS, ROWS), jnp.float32)],
        compiler_params=pltpu.CompilerParams(vmem_limit_bytes=24 * 2**20),
        cost_estimate=COST,
    )(place, *plains, *weights, *given)


def core_sum(sums):
    pair = lax.all_to_all(sums, "c", 0, 0, tiled=False)
    pair = pair.reshape(NC, NL, -1, GROUP, LANES)
    end = 4 * PIECE
    bound = jnp.maximum(pair[0, :, :, end:] + pair[1, :, :, end:], 1e-30)
    power = jnp.floor(jnp.log2(bound)) - 14
    scaled = (pair[0, :, :, :end] + pair[1, :, :, :end]) * jnp.exp2(-power[:, :, :1])
    return jnp.concatenate([scaled, power], axis=2).astype(jnp.float16)


def chip_sum(sums):
    n = sums.shape[1]
    sums = sums.reshape(NL, n * GROUP, LANES)
    got = lax.all_to_all(sums, ("y", "zh"), 0, 0, tiled=False)
    got = got.astype(jnp.float32).reshape(NL, n, GROUP, LANES)
    end = 4 * PIECE
    part = (got[..., :end, :] * jnp.exp2(got[..., end : end + 1, :])).sum(0)
    part = part.reshape(n, 2, 3, OWN, LANES)
    rest = part[:, :, 2].reshape(n, 2, OWN, 2, ROWS - LANES).swapaxes(2, 3)
    return jnp.concatenate([part[:, :, :2], rest], axis=-1).reshape(n, 4, OWN, ROWS)


def turned(value, steps):
    return lax.dynamic_slice_in_dim(jnp.concatenate([value, value]), steps, value.shape[0])


def per_device(grads, in_factor, out_factor):
    factor = 1.0 / math.sqrt(NL * NC * grads.shape[-1])
    z, x = lax.axis_index("zl"), lax.axis_index("x")
    tiles = factor_tiles(in_factor[0], out_factor[0])
    half = ROWS // 2
    p0 = grads[0]
    p1, p3 = moved(p0, "x", 1), moved(p0, "x", -1)
    p4 = lax.ppermute(p0, "zl", [(0, 2), (3, 1), (1, 0)])
    w0, own = weigh(p0, tiles, copied=True)
    p5 = lax.ppermute(own, "zl", [(0, 3), (2, 1), (3, 2)])
    p2 = jnp.concatenate([moved(p1[:half], "x", 1), moved(p3[half:], "x", -1)])
    w1, w2, w3, w4 = (weigh(p, tiles) for p in (p1, p2, p3, p4))
    early = products(
        [own, p1, p2, p3, p4],
        [w0, w1, w2, w3, w4],
        [
            (None, 0, None, (0, 0)),
            (1, 1, (1, 0), (0, 1)),
            (None, 0, None, (0, 2)),
            (None, 0, None, (4, 0)),
            (1, 1, (4, 1), (1, 4)),
            (1, 2, (4, 2), (2, 4)),
            (1, 3, (4, 3), (3, 4)),
            (None, 0, None, (0, 4)),
        ],
        [(0, 1, 2, 7), (3, 4, 5, 6)],
    )
    sums = products(
        [p4, p5],
        [w0, w1, w2, w3],
        [(0, 1, (0, r), (1, r)) for r in range(NX)],
        [tuple(range(NX))],
        early,
    )
    row, two, following = chip_sum(core_sum(sums))
    across = lax.ppermute(jnp.concatenate([row[3:], two[1:]]), "zl", [(1, 3), (2, 0)])
    middle = (z == 1) | (z == 2)
    other = [two[0]] + [jnp.where(x >= r, row[min(r, 2)], two[r]) for r in range(1, NX)]
    sent = turned(jnp.stack([following, jnp.stack(other)], axis=1)[::-1], (NX - 1 - x) % NX)
    sent, row, two, following = lax.optimization_barrier((sent, row, two, following))
    got = lax.all_to_all(sent, "x", 0, 0, tiled=False)
    got, across = lax.optimization_barrier((got, across))
    got = turned(got, x)
    two = jnp.where(middle, two, across)
    out = [None] * 9
    out[0], out[4], out[8] = row[0], following[0], two[0]
    for r in range(1, NX):
        inside = x + r < NX
        near = row[1] if r == 3 else got[r, 1]
        far = jnp.where(middle, got[r, 1], two[NX - r])
        out[r] = jnp.where(inside, near, got[r, 0])
        out[r + 4] = jnp.where(inside, got[r, 0], far)
    return (jnp.stack(out) * factor).transpose(2, 0, 1)


def solution(mesh):
    fine = Mesh(mesh.devices.reshape(NZ, NX, NY, NH, NC), ("zl", "x", "y", "zh", "c"))
    layer, group = ("y", "zh", "c"), ("zl", "x")
    in_specs = (P(layer, group, None), P(layer, None, None), P(layer, None, None))
    return jax.shard_map(
        per_device, mesh=fine, in_specs=in_specs, out_specs=P(group, None, layer), check_vma=False
    )
```

```python
import functools
import math

import jax
import jax.numpy as jnp
import numpy as np
from jax import lax
from jax.experimental import pallas as pl
from jax.experimental.pallas import tpu as pltpu
from jax.sharding import Mesh, PartitionSpec as P

NZ, NX, NY, NH, NC = 4, 4, 8, 2, 2
NL = NY * NH
ROWS = 192
OWN = ROWS // (NL * NC)
LANES = 128
PIECE = OWN * ROWS // LANES
GROUP = 40
TILE = 256
NN, NT = ((1,), (0,)), ((1,), (1,))
COST = pl.CostEstimate(flops=10**10, bytes_accessed=10**6, transcendentals=0)


def moved(value, axis, steps):
    count = lax.axis_size(axis)
    return lax.ppermute(value, axis, [(s, (s + steps) % count) for s in range(count)])


def spread():
    at = np.arange(TILE)
    six = np.arange(64)
    by_four = (at[:, None] // 4 == six).astype(np.float32)
    by_last = (at[:, None] % 64 == six).astype(np.float32)
    mixed = (at[:, None] // 16 * 4 + at[:, None] % 4 == six).astype(np.float32)
    inner = (at[:, None] % 4 == at // 64).astype(np.float32)
    outer = (at[:, None] // 4 % 4 == at // 4 % 4).astype(np.float32)
    order = np.zeros((TILE, TILE), np.float32)
    order[at, at % 64 * 4 + at // 64] = 1
    return [jnp.asarray(m) for m in (by_four, by_last, mixed, inner, outer)], jnp.asarray(
        order, jnp.bfloat16
    )


def tiles_kernel(in_ref, out_ref, four_ref, last_ref, mixed_ref, im_ref, om_ref, a_ref, b_ref):
    def exact(a, b, dims):
        return lax.dot_general(
            a,
            b,
            (dims, ((), ())),
            precision=lax.Precision.HIGHEST,
            preferred_element_type=jnp.float32,
        )

    def parts(ref, matrix):
        for part in range(3):
            rounded = matrix.astype(jnp.bfloat16)
            ref[:, part * TILE : (part + 1) * TILE] = rounded
            matrix = matrix - rounded.astype(jnp.float32)

    inner = exact(exact(four_ref[...], in_ref[...], NT), last_ref[...], NT)
    parts(a_ref, inner * im_ref[...])
    outer = exact(exact(mixed_ref[...], out_ref[...], NN), mixed_ref[...], NT)
    parts(b_ref, outer * om_ref[...])


def factor_tiles(in_mat, out_mat):
    matrices, order = spread()
    shape = jax.ShapeDtypeStruct((TILE, 3 * TILE), jnp.bfloat16)
    inner, outer = pl.pallas_call(
        tiles_kernel, out_shape=(shape, shape), cost_estimate=COST
    )(in_mat, out_mat, *matrices)
    return inner, outer, order


def dot(a, b, dims):
    return lax.dot_general(a, b, (dims, ((), ())), preferred_element_type=jnp.float32)


def weigh_kernel(p_ref, inner_ref, outer_ref, order_ref, w_ref, *rest):
    *copies, t_ref = rest
    tiles = p_ref.shape[1] // TILE
    for copy in copies:
        copy[...] = p_ref[...]

    @pl.loop(0, tiles, unroll=tiles)
    def _(b):
        x = p_ref[:, pl.ds(pl.multiple_of(b * TILE, TILE), TILE)]
        t_ref[b] = dot(inner_ref[...], jnp.concatenate([x] * 3, axis=1), NT)

    @pl.loop(0, tiles, unroll=tiles)
    def _(g):
        at = pl.ds(pl.multiple_of(g * 16, 16), 16)
        x = t_ref[:, at, :].reshape(TILE, ROWS)
        high = x.astype(jnp.bfloat16)
        low = (x - high.astype(jnp.float32)).astype(jnp.bfloat16)
        left = jnp.concatenate([outer_ref[:, : 2 * TILE], outer_ref[:, :TILE]], axis=1)
        y = dot(left, jnp.concatenate([high, high, low], axis=0), NN)
        t_ref[:, at, :] = y.reshape(16, 16, ROWS)

    @pl.loop(0, tiles, unroll=tiles)
    def _(b):
        y = dot(order_ref[...], t_ref[b].astype(jnp.bfloat16), NN)
        w_ref[pl.ds(pl.multiple_of(b * TILE, TILE), TILE), :] = y.astype(jnp.bfloat16)


def weigh(rows, tiles, copied=False):
    width = rows.shape[1]
    out = jax.ShapeDtypeStruct((width, ROWS), jnp.bfloat16)
    return pl.pallas_call(
        weigh_kernel,
        out_shape=(out, jax.ShapeDtypeStruct(rows.shape, rows.dtype)) if copied else out,
        scratch_shapes=[pltpu.VMEM((width // TILE, TILE, ROWS), jnp.float32)],
        compiler_params=pltpu.CompilerParams(vmem_limit_bytes=24 * 2**20),
        cost_estimate=COST,
    )(rows, *tiles)


def products_kernel(picks, groups, n_p, n_w, place_ref, *refs):
    p_refs, w_refs = refs[:n_p], refs[n_p : n_p + n_w]
    out_ref, total = refs[-2:]

    def score(slot, p, w):
        total[slot] = dot(p_refs[p][...], w_refs[w][...], NN)

    for slot, (axis, least, below, reached) in enumerate(picks):
        if axis is None:
            score(slot, *reached)
        else:
            here = place_ref[axis]
            pl.when(here < least)(functools.partial(score, slot, *below))
            pl.when(here >= least)(functools.partial(score, slot, *reached))
    top = jnp.full((NC, NL, GROUP - 4 * PIECE, LANES), jnp.max(jnp.abs(total[...])), jnp.float32)
    for group, slots in enumerate(groups):
        start = group * GROUP
        out_ref[:, :, start + 4 * PIECE : start + GROUP] = top
        for pair in range(2):
            a, b = total[slots[2 * pair]], total[slots[2 * pair + 1]]
            rest = jnp.concatenate([a[:, LANES:], b[:, LANES:]], axis=1)
            for n, piece in enumerate((a[:, :LANES], b[:, :LANES], rest)):
                to = start + (3 * pair + n) * OWN
                for chip in range(NL):
                    for core in range(NC):
                        at = (chip * NC + core) * OWN
                        out_ref[core, chip, to : to + OWN] = piece[at : at + OWN]


def products(plains, weights, picks, groups):
    place = jnp.stack([lax.axis_index("zl"), lax.axis_index("x")]).astype(jnp.int32)
    vmem = pl.BlockSpec(memory_space=pltpu.VMEM)
    height = len(groups) * GROUP
    return pl.pallas_call(
        functools.partial(products_kernel, picks, groups, len(plains), len(weights)),
        out_shape=jax.ShapeDtypeStruct((NC, NL, height, LANES), jnp.float32),
        in_specs=[pl.BlockSpec(memory_space=pltpu.SMEM)] + [vmem] * (len(plains) + len(weights)),
        out_specs=vmem,
        scratch_shapes=[pltpu.VMEM((len(picks), ROWS, ROWS), jnp.float32)],
        compiler_params=pltpu.CompilerParams(vmem_limit_bytes=24 * 2**20),
        cost_estimate=COST,
    )(place, *plains, *weights)


def core_sum(sums):
    pair = lax.all_to_all(sums, "c", 0, 0, tiled=False)
    pair = pair.reshape(NC, NL, -1, GROUP, LANES)
    end = 4 * PIECE
    bound = jnp.maximum(pair[0, :, :, end:] + pair[1, :, :, end:], 1e-30)
    power = jnp.floor(jnp.log2(bound)) - 14
    scaled = (pair[0, :, :, :end] + pair[1, :, :, :end]) * jnp.exp2(-power[:, :, :1])
    return jnp.concatenate([scaled, power], axis=2).astype(jnp.float16)


def chip_sum(sums):
    n = sums.shape[1]
    sums = sums.reshape(NL, n * GROUP, LANES)
    got = lax.all_to_all(sums, ("y", "zh"), 0, 0, tiled=False)
    got = got.astype(jnp.float32).reshape(NL, n, GROUP, LANES)
    end = 4 * PIECE
    part = (got[..., :end, :] * jnp.exp2(got[..., end : end + 1, :])).sum(0)
    part = part.reshape(n, 2, 3, OWN, LANES)
    rest = part[:, :, 2].reshape(n, 2, OWN, 2, ROWS - LANES).swapaxes(2, 3)
    return jnp.concatenate([part[:, :, :2], rest], axis=-1).reshape(n, 4, OWN, ROWS)


def turned(value, steps):
    return lax.dynamic_slice_in_dim(jnp.concatenate([value, value]), steps, value.shape[0])


def per_device(grads, in_factor, out_factor):
    factor = 1.0 / math.sqrt(NL * NC * grads.shape[-1])
    z, x = lax.axis_index("zl"), lax.axis_index("x")
    tiles = factor_tiles(in_factor[0], out_factor[0])
    half = ROWS // 2
    p0 = grads[0]
    p1, p3 = moved(p0, "x", 1), moved(p0, "x", -1)
    p4 = lax.ppermute(p0, "zl", [(0, 2), (3, 1), (1, 0)])
    w0, own = weigh(p0, tiles, copied=True)
    p5 = lax.ppermute(own, "zl", [(0, 3), (2, 1), (3, 2)])
    p2 = jnp.concatenate([moved(p1[:half], "x", 1), moved(p3[half:], "x", -1)])
    w1, w2, w3, w4 = (weigh(p, tiles) for p in (p1, p2, p3, p4))
    early = products(
        [own, p1, p2, p3, p4],
        [w0, w1, w2, w3, w4],
        [
            (None, 0, None, (0, 0)),
            (1, 1, (1, 0), (0, 1)),
            (None, 0, None, (0, 2)),
            (None, 0, None, (4, 0)),
            (1, 1, (4, 1), (1, 4)),
            (1, 2, (4, 2), (2, 4)),
            (1, 3, (4, 3), (3, 4)),
            (None, 0, None, (0, 4)),
        ],
        [(0, 1, 2, 7), (3, 4, 5, 6)],
    )
    late = products(
        [p4, p5],
        [w0, w1, w2, w3],
        [(0, 1, (0, r), (1, r)) for r in range(NX)],
        [tuple(range(NX))],
    )
    sums = jnp.concatenate([core_sum(early), core_sum(late)], axis=1)
    row, two, following = chip_sum(sums)
    across = lax.ppermute(jnp.concatenate([row[3:], two[1:]]), "zl", [(1, 3), (2, 0)])
    middle = (z == 1) | (z == 2)
    other = [two[0]] + [jnp.where(x >= r, row[min(r, 2)], two[r]) for r in range(1, NX)]
    sent = turned(jnp.stack([following, jnp.stack(other)], axis=1)[::-1], (NX - 1 - x) % NX)
    sent, row, two, following = lax.optimization_barrier((sent, row, two, following))
    got = lax.all_to_all(sent, "x", 0, 0, tiled=False)
    got, across = lax.optimization_barrier((got, across))
    got = turned(got, x)
    two = jnp.where(middle, two, across)
    out = [None] * 9
    out[0], out[4], out[8] = row[0], following[0], two[0]
    for r in range(1, NX):
        inside = x + r < NX
        near = row[1] if r == 3 else got[r, 1]
        far = jnp.where(middle, got[r, 1], two[NX - r])
        out[r] = jnp.where(inside, near, got[r, 0])
        out[r + 4] = jnp.where(inside, got[r, 0], far)
    return (jnp.stack(out) * factor).transpose(2, 0, 1)


def solution(mesh):
    fine = Mesh(mesh.devices.reshape(NZ, NX, NY, NH, NC), ("zl", "x", "y", "zh", "c"))
    layer, group = ("y", "zh", "c"), ("zl", "x")
    in_specs = (P(layer, group, None), P(layer, None, None), P(layer, None, None))
    return jax.shard_map(
        per_device, mesh=fine, in_specs=in_specs, out_specs=P(group, None, layer), check_vma=False
    )
```

```python
import functools
import math

import jax
import jax.numpy as jnp
import numpy as np
from jax import lax
from jax.experimental import pallas as pl
from jax.experimental.pallas import tpu as pltpu
from jax.sharding import Mesh, PartitionSpec as P

NZ, NX, NY, NH, NC = 4, 4, 8, 2, 2
NL = NY * NH
ROWS = 192
OWN = ROWS // (NL * NC)
LANES = 128
PIECE = OWN * ROWS // LANES
GROUP = 40
TILE = 256
NN, NT = ((1,), (0,)), ((1,), (1,))
COST = pl.CostEstimate(flops=10**10, bytes_accessed=10**6, transcendentals=0)


def moved(value, axis, steps):
    count = lax.axis_size(axis)
    return lax.ppermute(value, axis, [(s, (s + steps) % count) for s in range(count)])


def spread():
    at = np.arange(TILE)
    six = np.arange(64)
    by_four = (at[:, None] // 4 == six).astype(np.float32)
    by_last = (at[:, None] % 64 == six).astype(np.float32)
    mixed = (at[:, None] // 16 * 4 + at[:, None] % 4 == six).astype(np.float32)
    inner = (at[:, None] % 4 == at // 64).astype(np.float32)
    outer = (at[:, None] // 4 % 4 == at // 4 % 4).astype(np.float32)
    order = np.zeros((TILE, TILE), np.float32)
    order[at, at % 64 * 4 + at // 64] = 1
    return [jnp.asarray(m) for m in (by_four, by_last, mixed, inner, outer)], jnp.asarray(
        order, jnp.bfloat16
    )


def tiles_kernel(in_ref, out_ref, four_ref, last_ref, mixed_ref, im_ref, om_ref, a_ref, b_ref):
    def exact(a, b, dims):
        return lax.dot_general(
            a,
            b,
            (dims, ((), ())),
            precision=lax.Precision.HIGHEST,
            preferred_element_type=jnp.float32,
        )

    def parts(ref, matrix):
        for part in range(3):
            rounded = matrix.astype(jnp.bfloat16)
            ref[:, part * TILE : (part + 1) * TILE] = rounded
            matrix = matrix - rounded.astype(jnp.float32)

    inner = exact(exact(four_ref[...], in_ref[...], NT), last_ref[...], NT)
    parts(a_ref, inner * im_ref[...])
    outer = exact(exact(mixed_ref[...], out_ref[...], NN), mixed_ref[...], NT)
    parts(b_ref, outer * om_ref[...])


def factor_tiles(in_mat, out_mat):
    matrices, order = spread()
    shape = jax.ShapeDtypeStruct((TILE, 3 * TILE), jnp.bfloat16)
    inner, outer = pl.pallas_call(
        tiles_kernel, out_shape=(shape, shape), cost_estimate=COST
    )(in_mat, out_mat, *matrices)
    return inner, outer, order


def dot(a, b, dims):
    return lax.dot_general(a, b, (dims, ((), ())), preferred_element_type=jnp.float32)


def weigh_kernel(unused, p_ref, inner_ref, outer_ref, order_ref, *rest):
    w_ref, *copies, t_ref = rest[unused:]
    tiles = p_ref.shape[1] // TILE
    for copy in copies:
        copy[...] = p_ref[...]

    @pl.loop(0, tiles, unroll=tiles)
    def _(b):
        x = p_ref[:, pl.ds(pl.multiple_of(b * TILE, TILE), TILE)]
        t_ref[b] = dot(inner_ref[...], jnp.concatenate([x] * 3, axis=1), NT)

    @pl.loop(0, tiles, unroll=tiles)
    def _(g):
        at = pl.ds(pl.multiple_of(g * 16, 16), 16)
        x = t_ref[:, at, :].reshape(TILE, ROWS)
        high = x.astype(jnp.bfloat16)
        low = (x - high.astype(jnp.float32)).astype(jnp.bfloat16)
        left = jnp.concatenate([outer_ref[:, : 2 * TILE], outer_ref[:, :TILE]], axis=1)
        y = dot(left, jnp.concatenate([high, high, low], axis=0), NN)
        t_ref[:, at, :] = y.reshape(16, 16, ROWS)

    @pl.loop(0, tiles, unroll=tiles)
    def _(b):
        y = dot(order_ref[...], t_ref[b].astype(jnp.bfloat16), NN)
        w_ref[pl.ds(pl.multiple_of(b * TILE, TILE), TILE), :] = y.astype(jnp.bfloat16)


def weigh(rows, tiles, copied=False, later=()):
    width = rows.shape[1]
    out = jax.ShapeDtypeStruct((width, ROWS), jnp.bfloat16)
    return pl.pallas_call(
        functools.partial(weigh_kernel, len(later)),
        out_shape=(out, jax.ShapeDtypeStruct(rows.shape, rows.dtype)) if copied else out,
        in_specs=[pl.BlockSpec(memory_space=pltpu.VMEM)] * (1 + len(tiles))
        + [pl.BlockSpec(memory_space=pl.ANY)] * len(later),
        scratch_shapes=[pltpu.VMEM((width // TILE, TILE, ROWS), jnp.float32)],
        compiler_params=pltpu.CompilerParams(vmem_limit_bytes=24 * 2**20),
        cost_estimate=COST,
    )(rows, *tiles, *later)


def products_kernel(picks, groups, n_p, n_w, place_ref, *refs):
    p_refs, w_refs = refs[:n_p], refs[n_p : n_p + n_w]
    given, (out_ref, total) = refs[n_p + n_w : -2], refs[-2:]
    first = 0
    if given:
        first = given[0].shape[2]
        out_ref[:, :, :first] = given[0][...]

    def score(slot, p, w):
        total[slot] = dot(p_refs[p][...], w_refs[w][...], NN)

    for slot, (axis, least, below, reached) in enumerate(picks):
        if axis is None:
            score(slot, *reached)
        else:
            here = place_ref[axis]
            pl.when(here < least)(functools.partial(score, slot, *below))
            pl.when(here >= least)(functools.partial(score, slot, *reached))
    top = jnp.full((NC, NL, GROUP - 4 * PIECE, LANES), jnp.max(jnp.abs(total[...])), jnp.float32)
    for group, slots in enumerate(groups):
        start = first + group * GROUP
        out_ref[:, :, start + 4 * PIECE : start + GROUP] = top
        for pair in range(2):
            a, b = total[slots[2 * pair]], total[slots[2 * pair + 1]]
            rest = jnp.concatenate([a[:, LANES:], b[:, LANES:]], axis=1)
            for n, piece in enumerate((a[:, :LANES], b[:, :LANES], rest)):
                to = start + (3 * pair + n) * OWN
                for chip in range(NL):
                    for core in range(NC):
                        at = (chip * NC + core) * OWN
                        out_ref[core, chip, to : to + OWN] = piece[at : at + OWN]


def products(plains, weights, picks, groups, sums=None):
    place = jnp.stack([lax.axis_index("zl"), lax.axis_index("x")]).astype(jnp.int32)
    vmem = pl.BlockSpec(memory_space=pltpu.VMEM)
    given = () if sums is None else (sums,)
    height = sum(v.shape[2] for v in given) + len(groups) * GROUP
    return pl.pallas_call(
        functools.partial(products_kernel, picks, groups, len(plains), len(weights)),
        out_shape=jax.ShapeDtypeStruct((NC, NL, height, LANES), jnp.float32),
        in_specs=[pl.BlockSpec(memory_space=pltpu.SMEM)] + [vmem] * (len(plains) + len(weights) + len(given)),
        out_specs=vmem,
        scratch_shapes=[pltpu.VMEM((len(picks), ROWS, ROWS), jnp.float32)],
        compiler_params=pltpu.CompilerParams(vmem_limit_bytes=24 * 2**20),
        cost_estimate=COST,
    )(place, *plains, *weights, *given)


def core_sum(sums):
    pair = lax.all_to_all(sums, "c", 0, 0, tiled=False)
    pair = pair.reshape(NC, NL, -1, GROUP, LANES)
    end = 4 * PIECE
    bound = jnp.maximum(pair[0, :, :, end:] + pair[1, :, :, end:], 1e-30)
    power = jnp.floor(jnp.log2(bound)) - 14
    scaled = (pair[0, :, :, :end] + pair[1, :, :, :end]) * jnp.exp2(-power[:, :, :1])
    return jnp.concatenate([scaled, power], axis=2).astype(jnp.float16)


def chip_sum(sums):
    n = sums.shape[1]
    sums = sums.reshape(NL, n * GROUP, LANES)
    got = lax.all_to_all(sums, ("y", "zh"), 0, 0, tiled=False)
    got = got.astype(jnp.float32).reshape(NL, n, GROUP, LANES)
    end = 4 * PIECE
    part = (got[..., :end, :] * jnp.exp2(got[..., end : end + 1, :])).sum(0)
    part = part.reshape(n, 2, 3, OWN, LANES)
    rest = part[:, :, 2].reshape(n, 2, OWN, 2, ROWS - LANES).swapaxes(2, 3)
    return jnp.concatenate([part[:, :, :2], rest], axis=-1).reshape(n, 4, OWN, ROWS)


def turned(value, steps):
    return lax.dynamic_slice_in_dim(jnp.concatenate([value, value]), steps, value.shape[0])


def per_device(grads, in_factor, out_factor):
    factor = 1.0 / math.sqrt(NL * NC * grads.shape[-1])
    z, x = lax.axis_index("zl"), lax.axis_index("x")
    tiles = factor_tiles(in_factor[0], out_factor[0])
    half = ROWS // 2
    p0 = grads[0]
    p1, p3 = moved(p0, "x", 1), moved(p0, "x", -1)
    p4 = lax.ppermute(p0, "zl", [(0, 2), (3, 1), (1, 0)])
    w0, own = weigh(p0, tiles, copied=True)
    p5 = lax.ppermute(own, "zl", [(0, 3), (2, 1), (3, 2)])
    p2 = jnp.concatenate([moved(p1[:half], "x", 1), moved(p3[half:], "x", -1)])
    w4 = weigh(p4, tiles)
    w1, w3 = (weigh(p, tiles, later=(w4,)) for p in (p1, p3))
    w2 = weigh(p2, tiles)
    early = products(
        [own, p1, p2, p3, p4],
        [w0, w1, w2, w3, w4],
        [
            (None, 0, None, (0, 0)),
            (1, 1, (1, 0), (0, 1)),
            (None, 0, None, (0, 2)),
            (None, 0, None, (4, 0)),
            (1, 1, (4, 1), (1, 4)),
            (1, 2, (4, 2), (2, 4)),
            (1, 3, (4, 3), (3, 4)),
            (None, 0, None, (0, 4)),
        ],
        [(0, 1, 2, 7), (3, 4, 5, 6)],
    )
    sums = products(
        [p4, p5],
        [w0, w1, w2, w3],
        [(0, 1, (0, r), (1, r)) for r in range(NX)],
        [tuple(range(NX))],
        early,
    )
    row, two, following = chip_sum(core_sum(sums))
    across = lax.ppermute(jnp.concatenate([row[3:], two[1:]]), "zl", [(1, 3), (2, 0)])
    middle = (z == 1) | (z == 2)
    other = [two[0]] + [jnp.where(x >= r, row[min(r, 2)], two[r]) for r in range(1, NX)]
    sent = turned(jnp.stack([following, jnp.stack(other)], axis=1)[::-1], (NX - 1 - x) % NX)
    sent, row, two, following = lax.optimization_barrier((sent, row, two, following))
    got = lax.all_to_all(sent, "x", 0, 0, tiled=False)
    got, across = lax.optimization_barrier((got, across))
    got = turned(got, x)
    two = jnp.where(middle, two, across)
    out = [None] * 9
    out[0], out[4], out[8] = row[0], following[0], two[0]
    for r in range(1, NX):
        inside = x + r < NX
        near = row[1] if r == 3 else got[r, 1]
        far = jnp.where(middle, got[r, 1], two[NX - r])
        out[r] = jnp.where(inside, near, got[r, 0])
        out[r + 4] = jnp.where(inside, got[r, 0], far)
    return (jnp.stack(out) * factor).transpose(2, 0, 1)


def solution(mesh):
    fine = Mesh(mesh.devices.reshape(NZ, NX, NY, NH, NC), ("zl", "x", "y", "zh", "c"))
    layer, group = ("y", "zh", "c"), ("zl", "x")
    in_specs = (P(layer, group, None), P(layer, None, None), P(layer, None, None))
    return jax.shard_map(
        per_device, mesh=fine, in_specs=in_specs, out_specs=P(group, None, layer), check_vma=False
    )
```
